512 devices in a mesh: grp: 16 (over z, core), pt: 32 (over x, y).
Axes of the slice: x: 4, y: 8, z: 8, core: 2. Of those that a mesh axis runs over, the one named last changes fastest.
Arguments:
- features: bfloat16 [262144, 512], P(('grp', 'pt')), as said below
- cotangent: bfloat16 [262144, 512], P(('grp', 'pt')), may hold values from -6 to 6
- conv_weight: float32 [27, 512], replicated, may hold values from -1.5 to 1.5
- neighbours: int32 [262144, 27], P(('grp', 'pt')), may hold values from -1 to 639, as said below
- halo_index: int32 [512, 128], P(('grp', 'pt')), may hold values from 0 to 511, as said below
- send_index: int32 [512, 32, 32], P(('grp', 'pt')), may hold values from -1 to 511, as said below
- curve_slot: int32 [262144], P(('grp', 'pt')), may hold values from 0 to 1023, as said below
Outputs:
- grad_features: bfloat16 [262144, 512], P(('grp', 'pt'))
- grad_conv: float32 [27, 512], replicated
The draws below stay inside these ranges and needn't reach their ends.
Inputs may be any that keep to these rules, and one draw needn't show every extreme that they name: `features`: each feature lies within -10 to 10. `neighbours`: offset 27 // 2 names the point itself; other entries name own rows, borrowed rows (512 and up) or -1. `halo_index`: the 64 rows of each half are distinct. `send_index`: for every tile and curve shard the used slots come first and the rest hold -1; a tile sends each of its rows exactly once; every tile fills all 32 slots for one curve shard, and every curve shard receives 512 rows. `curve_slot`: within each curve shard every used slot appears once.
All inputs are finite; a program needn't handle non-finite values.
Results may differ from the reference program's by a relative error of at most 0.0045.
The reference program's roundings to bfloat16 on the way (of `padded`, `hidden`, `curve`, `probs_low`, `dscores`, `grad_curve` and `grad_hidden`) count: a program that leaves them out, or rounds other values in their place, can miss the bound.
Values may be sent and summed in bfloat16 or wider, within the bound.
A program may use at most 64 MiB of HBM per device.

```python
import jax
import jax.numpy as jnp
from jax import lax

D = 512
HEADS = 32
PATCH = 512
TAPS = 27
ROWS = 512
RIM = 64
SLOTS = 32
TILES = 512
POINTS = 262144
N_GRP = 16
N_PT = 32


def relay_tables(key):

    def one_region(region_key):
        key_spread, key_weights, key_order, key_shuffle = jax.random.split(region_key, 4)
        remain = ROWS - SLOTS
        base = remain // (N_PT - 1)
        leftover = remain - base * (N_PT - 1)
        paired = (N_PT - 1) // 2
        unpaired = N_PT - 1 - 2 * paired
        spread = jax.random.randint(key_spread, (paired,), 0, max(base, 1)).astype(jnp.int32)
        moves = jnp.concatenate([spread, -spread, jnp.zeros((unpaired,), jnp.int32)])
        others = base + moves + (jnp.arange(N_PT - 1) < leftover).astype(jnp.int32)
        weights = jnp.concatenate([jnp.full((1,), SLOTS, jnp.int32), others.astype(jnp.int32)])
        weights = jax.random.permutation(key_weights, weights)
        source_ids = jnp.arange(N_PT)[:, None]
        target_ids = jnp.arange(N_PT)[None, :]
        counts = weights[(target_ids - source_ids) % N_PT]
        starts = jnp.cumsum(counts, axis=1) - counts
        orders = jax.vmap(lambda one_key: jax.random.permutation(one_key, ROWS))(jax.random.split(key_order, N_PT))
        slot_ids = jnp.arange(SLOTS)
        positions = jnp.minimum(starts[:, :, None] + slot_ids, ROWS - 1)
        live = slot_ids < counts[:, :, None]
        picked = orders[jnp.arange(N_PT)[:, None, None], positions]
        sending = jnp.where(live, picked, -1).astype(jnp.int32)
        live_curve = jnp.transpose(live, (1, 0, 2)).reshape(N_PT, N_PT * SLOTS).astype(jnp.int32)
        ranked = jnp.argsort(1 - live_curve, axis=1, stable=True)[:, :ROWS]
        shuffles = jax.vmap(lambda one_key: jax.random.permutation(one_key, ROWS))(jax.random.split(key_shuffle, N_PT))
        curve = jnp.take_along_axis(ranked, shuffles, axis=1).astype(jnp.int32)
        return (sending, curve)
    region_keys = jax.vmap(lambda region: jax.random.fold_in(key, region))(jnp.arange(N_GRP))
    sending, curve = jax.vmap(one_region)(region_keys)
    return (sending.reshape(N_GRP * N_PT, N_PT, SLOTS), curve.reshape(N_GRP * N_PT * ROWS))


def draw_send_index(key, part):
    tables = relay_tables(key)
    return tables[0]


def draw_curve_slot(key, part):
    tables = relay_tables(key)
    return tables[1]


def draw_neighbours(key, part):
    key = jax.random.fold_in(key, 5)
    key_kind, key_own, key_rim = jax.random.split(key, 3)
    kinds = jax.random.randint(key_kind, (POINTS, TAPS), 0, 20)
    own_rows = jax.random.randint(key_own, (POINTS, TAPS), 0, ROWS)
    rim_rows = jax.random.randint(key_rim, (POINTS, TAPS), ROWS, ROWS + 2 * RIM)
    values = jnp.where(kinds < 6, -1, jnp.where(kinds < 9, rim_rows, own_rows))
    centre = (jnp.arange(POINTS) % ROWS).astype(jnp.int32)
    values = values.at[:, TAPS // 2].set(centre)
    return values.astype(jnp.int32)


def draw_halo_index(key, part):
    key = jax.random.fold_in(key, 7)
    tile_keys = jax.random.split(key, TILES)
    lists = jax.vmap(lambda one_key: jax.random.permutation(one_key, ROWS)[:2 * RIM])(tile_keys)
    return lists.astype(jnp.int32)


def draw_features(key, part):
    key = jax.random.fold_in(key, 11)
    values = jnp.clip(jax.random.normal(key, (POINTS, D), jnp.float32), -4.0, 4.0)
    return values.astype(jnp.bfloat16)


def block_levels(rng, shape, shards, smallest, high):
    factor_of = 1.0
    for position, blocks in shards:
        heights = jax.random.uniform(jax.random.fold_in(jax.random.fold_in(rng, 6), position), (blocks,), jnp.float32, smallest / len(shards), high / len(shards))
        factor_of = factor_of * jnp.repeat(jnp.exp(heights), shape[position] // blocks).reshape((-1,) + (1,) * (len(shape) - 1 - position))
    return factor_of


def gaussian(rng, dims, scale, limit, pieces=(), kind=jnp.bfloat16):
    array = jax.random.normal(rng, dims, jnp.float32) * scale
    if len(pieces) > 0:
        array = block_levels(rng, dims, pieces, -0.22, 0.18) * array
    return jnp.clip(array, min=-limit, max=limit).astype(kind)


def setup_inputs(seed: int = 0) -> dict:
    seeds = jax.random.split(jax.random.key(seed), 8)
    return {
        "features": draw_features(jax.random.fold_in(seeds[7], 71), 0),
        "cotangent": gaussian(seeds[1], (POINTS, D), 1.0, 6.0, ((0, 512),)),
        "conv_weight": gaussian(seeds[2], (TAPS, D), 0.25, 1.5, (), jnp.float32),
        "neighbours": draw_neighbours(jax.random.fold_in(seeds[7], 71), 0),
        "halo_index": draw_halo_index(jax.random.fold_in(seeds[7], 71), 0),
        "send_index": draw_send_index(jax.random.fold_in(seeds[7], 71), 0),
        "curve_slot": draw_curve_slot(jax.random.fold_in(seeds[7], 71), 0),
    }


def conv_forward(padded, tap_index, conv_weight):
    row_count = tap_index.shape[0]

    def add_tap(kernel_tap, accum):
        picked = padded[tap_index[:, kernel_tap]].astype(jnp.float32)
        return accum + conv_weight[kernel_tap] * picked
    start_value = jnp.zeros((row_count, padded.shape[1]), jnp.float32)
    summed = lax.fori_loop(0, conv_weight.shape[0], add_tap, start_value)
    return (padded[:row_count].astype(jnp.float32) + summed).astype(jnp.bfloat16)

def conv_backward(padded, tap_index, grad_rows, conv_weight):
    grad_float = grad_rows.astype(jnp.float32)

    def add_tap(kernel_tap, carry):
        spread, terms = carry
        picked = tap_index[:, kernel_tap]
        spread = spread.at[picked].add(conv_weight[kernel_tap] * grad_float)
        terms = terms.at[kernel_tap].set(lax.optimization_barrier(jnp.sum(grad_float * padded[picked].astype(jnp.float32), axis=0)))
        return (spread, terms)
    start_value = (jnp.zeros(padded.shape, jnp.float32), jnp.zeros(conv_weight.shape, jnp.float32))
    return lax.fori_loop(0, conv_weight.shape[0], add_tap, start_value)

def patch_grad(curve_patch, cot_patch):
    head_dim = D // HEADS
    scale = head_dim ** (-0.5)
    queries = curve_patch.reshape(PATCH, HEADS, head_dim).astype(jnp.float32)
    upstream = cot_patch.reshape(PATCH, HEADS, head_dim).astype(jnp.float32)
    scores = jnp.einsum('qhd,khd->hqk', queries, queries) * scale
    probs = jax.nn.softmax(scores, axis=-1)
    probs_low = lax.optimization_barrier(probs.astype(jnp.bfloat16)).astype(jnp.float32)
    dvalue = jnp.einsum('hqk,qhd->khd', probs_low, upstream)
    dprobs = jnp.einsum('qhd,khd->hqk', upstream, queries)
    delta = lax.optimization_barrier(jnp.sum(probs * dprobs, axis=-1, keepdims=True))
    dscores = lax.optimization_barrier((probs * (dprobs - delta)).astype(jnp.bfloat16)).astype(jnp.float32)
    dquery = jnp.einsum('hqk,khd->qhd', dscores, queries) * scale
    dkey = jnp.einsum('hqk,qhd->khd', dscores, queries) * scale
    grads = (dquery + dkey + dvalue).reshape(PATCH, D)
    return (cot_patch.astype(jnp.float32) + grads).astype(jnp.bfloat16)

def reference(features, cotangent, conv_weight, neighbours, halo_index, send_index, curve_slot):
    regions = N_GRP
    peer_count = N_PT
    table_rows = ROWS + 2 * RIM + 1
    tiled = features.reshape(regions, peer_count, ROWS, D)
    lent_index = halo_index.reshape(regions, peer_count, 2 * RIM)
    lent = jnp.take_along_axis(tiled, lent_index[..., None], axis=2)
    zero_rim = jnp.zeros((1, peer_count, RIM, D), jnp.bfloat16)
    from_prev = jnp.concatenate([zero_rim, lent[:-1, :, RIM:]], axis=0)
    from_next = jnp.concatenate([lent[1:, :, :RIM], zero_rim], axis=0)
    zero_row = jnp.zeros((regions, peer_count, 1, D), jnp.bfloat16)
    padded = jnp.concatenate([tiled, from_prev, from_next, zero_row], axis=2).reshape(TILES, table_rows, D)
    tap_index = jnp.where(neighbours < 0, ROWS + 2 * RIM, neighbours).astype(jnp.int32).reshape(TILES, ROWS, TAPS)
    hidden = lax.map(lambda pair_in: conv_forward(pair_in[0], pair_in[1], conv_weight), (padded, tap_index))
    sender_table = send_index.reshape(regions, peer_count, peer_count, SLOTS)
    slot_table = curve_slot.reshape(regions, peer_count, ROWS)
    source_tile = (slot_table // SLOTS).astype(jnp.int32)
    source_slot = (slot_table % SLOTS).astype(jnp.int32)
    region_ids = jnp.arange(regions, dtype=jnp.int32)[:, None, None]
    shard_ids = jnp.arange(peer_count, dtype=jnp.int32)[None, :, None]
    source_row = source_tile * ROWS + sender_table[region_ids, source_tile, shard_ids, source_slot]
    source_row = source_row.reshape(regions, peer_count * ROWS).astype(jnp.int32)
    hidden_regions = hidden.reshape(regions, peer_count * ROWS, D)
    curve = jnp.take_along_axis(hidden_regions, source_row[..., None], axis=1).reshape(POINTS, D)
    patch_count = POINTS // PATCH
    grad_curve = lax.map(lambda pair_in: patch_grad(pair_in[0], pair_in[1]), (curve.reshape(patch_count, PATCH, D), cotangent.reshape(patch_count, PATCH, D)))
    grad_curve = grad_curve.reshape(regions, peer_count * ROWS, D)
    empty = jnp.zeros((regions, peer_count * ROWS, D), jnp.bfloat16)
    grad_hidden = jax.vmap(lambda base, where_to, values: base.at[where_to].set(values))(empty, source_row, grad_curve)
    grad_hidden = grad_hidden.reshape(TILES, ROWS, D)
    spread, terms = lax.map(lambda trio: conv_backward(trio[0], trio[1], trio[2], conv_weight), (padded, tap_index, grad_hidden))
    own_part = spread[:, :ROWS]
    back_prev = spread[:, ROWS:ROWS + RIM].reshape(regions, peer_count, RIM, D)
    back_next = spread[:, ROWS + RIM:ROWS + 2 * RIM].reshape(regions, peer_count, RIM, D)
    zero_back = jnp.zeros((1, peer_count, RIM, D), jnp.float32)
    into_from_next = jnp.concatenate([back_prev[1:], zero_back], axis=0).reshape(TILES, RIM, D)
    into_from_prev = jnp.concatenate([zero_back, back_next[:-1]], axis=0).reshape(TILES, RIM, D)
    grad_total = grad_hidden.astype(jnp.float32) + own_part
    lent_flat = halo_index.reshape(TILES, 2 * RIM)

    def add_rims(tile_grad, tile_lent, prev_terms, next_terms):
        return tile_grad.at[tile_lent[:RIM]].add(prev_terms).at[tile_lent[RIM:]].add(next_terms)
    grad_total = jax.vmap(add_rims)(grad_total, lent_flat, into_from_prev, into_from_next)
    grad_features = grad_total.astype(jnp.bfloat16).reshape(POINTS, D)
    grad_conv = lax.optimization_barrier(jnp.sum(terms, axis=0))
    return (grad_features, grad_conv)
```

```python
import functools

import jax
import jax.numpy as jnp
from jax import lax
from jax.experimental import pallas as pl
from jax.experimental.pallas import tpu as pltpu
from jax.sharding import PartitionSpec as P

D = 512
ROWS = 512
RIM = 64
TABLE = ROWS + 2 * RIM
TAPS = 27
CENTRE = TAPS // 2
HEAD_DIM = 16
LANES = 128
BF16 = jnp.bfloat16
F32 = jnp.float32
I16 = jnp.int16
VMEM = pl.BlockSpec(memory_space=pltpu.VMEM)
MESH = pl.DeviceIdType.MESH


def dot(a, b, dims=((1,), (0,))):
    return lax.dot_general(a, b, (dims, ((), ())), preferred_element_type=F32)


def pick(mask):
    return jnp.where(mask, jnp.ones((), BF16), jnp.zeros((), BF16))


def rows_of(index_row, width):
    count = index_row.shape[1]
    column = jnp.broadcast_to(index_row, (LANES, count)).T.astype(I16)
    lane = lax.broadcasted_iota(jnp.int32, (count, LANES), 1).astype(I16)
    blocks = [pick(column == lane + jnp.asarray(start, I16)) for start in range(0, width, LANES)]
    return jnp.concatenate(blocks, axis=1)


def columns_of(index_row, height):
    count = index_row.shape[1]
    row = jnp.broadcast_to(index_row, (16, count)).astype(I16)
    sub = lax.broadcasted_iota(jnp.int32, (16, count), 0).astype(I16)
    blocks = [pick(row == sub + jnp.asarray(start, I16)) for start in range(0, height, 16)]
    return jnp.concatenate(blocks, axis=0)


def lend_kernel(halo_ref, features_ref, lent_ref):
    lent_ref[...] = dot(rows_of(halo_ref[...], ROWS), features_ref[...]).astype(BF16)


def other_tap(step):
    return jnp.where(step < CENTRE, step, step + 1)


def forward_kernel(taps_ref, weight_ref, send_ref, padded_ref, out_ref, acc_ref):
    own = padded_ref[:ROWS, :].astype(F32)
    acc_ref[...] = own + own * weight_ref[CENTRE : CENTRE + 1, :]

    def tap(step, _):
        k = other_tap(step)
        picked = dot(rows_of(taps_ref[pl.ds(k, 1), :], TABLE), padded_ref[...])
        acc_ref[...] += picked * weight_ref[pl.ds(k, 1), :]
        return 0

    lax.fori_loop(0, TAPS - 1, tap, 0)
    hidden = acc_ref[...].astype(BF16)
    out_ref[...] = dot(rows_of(send_ref[...], ROWS), hidden).astype(BF16)


def attention_kernel(curve_ref, cotangent_ref, slots_ref, out_ref, rows_ref, grad_ref):
    rows_ref[...] = dot(rows_of(curve_ref[...], slots_ref.shape[0]), slots_ref[...]).astype(BF16)

    def group(g, _):
        span = pl.ds(pl.multiple_of(g * LANES, LANES), LANES)
        rows = rows_ref[:, span]
        cot = cotangent_ref[:, span]
        scaled = rows * jnp.asarray(HEAD_DIM**-0.5, BF16)
        head_of = lax.broadcasted_iota(jnp.int32, (ROWS, LANES), 1) // HEAD_DIM
        total = cot.astype(F32)
        for h in range(LANES // HEAD_DIM):
            inside = head_of == h
            keys = jnp.where(inside, rows, jnp.zeros((), BF16))
            scores = dot(keys, scaled, ((1,), (1,)))
            dprobs = dot(keys, cot, ((1,), (1,)))
            weights = jnp.exp(scores - jnp.max(scores, axis=0, keepdims=True))
            probs = weights * (1.0 / jnp.sum(weights, axis=0, keepdims=True))
            delta = jnp.sum(probs * dprobs, axis=0, keepdims=True)
            dscores = (probs * (dprobs - delta)).astype(BF16)
            grads = dot(probs.astype(BF16), cot) + dot(dscores, scaled)
            grads = grads + dot(dscores, scaled, ((0,), (0,)))
            total = total + jnp.where(inside, grads, 0.0)
        grad_ref[:, span] = total.astype(BF16)
        return 0

    lax.fori_loop(0, D // LANES, group, 0)
    out_ref[...] = dot(columns_of(curve_ref[...], slots_ref.shape[0]), grad_ref[...]).astype(BF16)


def backward_kernel(
    taps_ref, weight_ref, send_ref, padded_ref, slots_ref, total_ref, rim_ref, terms_ref, grad_ref, spread_ref
):
    grad_ref[...] = dot(columns_of(send_ref[...], ROWS), slots_ref[...]).astype(BF16)
    grad = grad_ref[...].astype(F32)
    spread_ref[:ROWS, :] = grad + grad * weight_ref[CENTRE : CENTRE + 1, :]
    spread_ref[ROWS:, :] = jnp.zeros((2 * RIM, D), F32)
    terms_ref[CENTRE] = jnp.sum(grad * padded_ref[:ROWS, :].astype(F32), axis=0, keepdims=True)

    def tap(step, _):
        k = other_tap(step)
        landed = dot(columns_of(taps_ref[pl.ds(k, 1), :], TABLE), grad_ref[...])
        spread_ref[...] += landed * weight_ref[pl.ds(k, 1), :]
        terms_ref[k] = jnp.sum(landed * padded_ref[...].astype(F32), axis=0, keepdims=True)
        return 0

    lax.fori_loop(0, TAPS - 1, tap, 0)
    total_ref[...] = spread_ref[:ROWS, :]
    rim_ref[...] = spread_ref[ROWS:, :].astype(BF16)


def finish_kernel(halo_ref, total_ref, echoed_ref, out_ref):
    landed = dot(columns_of(halo_ref[...], ROWS), echoed_ref[...])
    out_ref[...] = (total_ref[...] + landed).astype(BF16)


def reduce_kernel(
    regions, peers, terms_ref, out_ref, parts, part, sums, whole, send_sem, part_sem, sum_sem, whole_sem
):
    grp = lax.axis_index("grp")
    me = lax.axis_index("pt")
    barrier = pltpu.get_barrier_semaphore()

    def greet_peer(step, _):
        peer = (me + step) % peers
        pl.semaphore_signal(barrier, inc=1, device_id=(grp, peer), device_id_type=MESH)
        return 0

    def greet_region(step, _):
        other = (grp + step) % regions
        pl.semaphore_signal(barrier, inc=1, device_id=(other, me), device_id_type=MESH)
        return 0

    lax.fori_loop(1, peers, greet_peer, 0)
    lax.fori_loop(1, regions, greet_region, 0)
    pl.semaphore_wait(barrier, peers - 1 + regions - 1)

    def to_owner(step):
        peer = (me + step) % peers
        return peer, pltpu.make_async_remote_copy(
            src_ref=terms_ref.at[peer % TAPS],
            dst_ref=parts.at[me],
            send_sem=send_sem.at[peer],
            recv_sem=part_sem.at[me],
            device_id=(grp, peer),
            device_id_type=MESH,
        )

    def from_peer(step):
        peer = (me + peers - step) % peers
        return pltpu.make_async_remote_copy(
            src_ref=terms_ref.at[0],
            dst_ref=parts.at[peer],
            send_sem=send_sem.at[peer],
            recv_sem=part_sem.at[peer],
            device_id=(grp, peer),
            device_id_type=MESH,
        )

    def to_region(step):
        other = (grp + step) % regions
        return pltpu.make_async_remote_copy(
            src_ref=part,
            dst_ref=sums.at[grp],
            send_sem=send_sem.at[peers + other],
            recv_sem=sum_sem.at[grp],
            device_id=(other, me),
            device_id_type=MESH,
        )

    def from_region(step):
        other = (grp + regions - step) % regions
        return pltpu.make_async_remote_copy(
            src_ref=part,
            dst_ref=sums.at[other],
            send_sem=send_sem.at[peers + other],
            recv_sem=sum_sem.at[other],
            device_id=(other, me),
            device_id_type=MESH,
        )

    def to_all(step):
        peer = (me + step) % peers
        return pltpu.make_async_remote_copy(
            src_ref=whole.at[me],
            dst_ref=whole.at[me],
            send_sem=send_sem.at[peers + regions + peer],
            recv_sem=whole_sem.at[me],
            device_id=(grp, peer),
            device_id_type=MESH,
        )

    def from_owner(peer):
        return pltpu.make_async_remote_copy(
            src_ref=whole.at[peer],
            dst_ref=whole.at[peer],
            send_sem=send_sem.at[peers + regions + peer],
            recv_sem=whole_sem.at[peer],
            device_id=(grp, peer),
            device_id_type=MESH,
        )

    def each(first, last, act):
        def step(i, _):
            act(i)
            return 0

        lax.fori_loop(first, last, step, 0)

    def start_term(step):
        peer, copy = to_owner(step)
        pl.when(peer < TAPS)(copy.start)

    each(1, peers, start_term)

    @pl.when(me < TAPS)
    def _():
        parts[me] = terms_ref[me]
        each(1, peers, lambda step: from_peer(step).wait_recv())
        mine = jnp.sum(parts[...], axis=0)
        part[...] = mine
        sums[grp] = mine
        each(1, regions, lambda step: to_region(step).start())
        each(1, regions, lambda step: from_region(step).wait_recv())
        whole[me] = jnp.sum(sums[...], axis=0)
        each(1, peers, lambda step: to_all(step).start())

    def take(owner):
        @pl.when(owner != me)
        def _():
            from_owner(owner).wait_recv()

    each(0, TAPS, take)

    def end_term(step):
        peer, copy = to_owner(step)
        pl.when(peer < TAPS)(copy.wait_send)

    each(1, peers, end_term)

    @pl.when(me < TAPS)
    def _():
        each(1, regions, lambda step: to_region(step).wait_send())
        each(1, peers, lambda step: to_all(step).wait_send())

    for k in range(TAPS):
        out_ref[k : k + 1, :] = whole[k]


def params(**more):
    return pltpu.CompilerParams(vmem_limit_bytes=48 * 2**20, **more)


def local(kernel, out_shape, scratch, *args):
    return pl.pallas_call(
        kernel,
        out_shape=out_shape,
        in_specs=[VMEM] * len(args),
        out_specs=jax.tree.map(lambda _: VMEM, out_shape),
        scratch_shapes=scratch,
        compiler_params=params(),
    )(*args)


def shape(dims, dtype=BF16):
    return jax.ShapeDtypeStruct(dims, dtype)


def total_terms(regions, peers, terms):
    return pl.pallas_call(
        functools.partial(reduce_kernel, regions, peers),
        out_shape=shape((TAPS, D), F32),
        in_specs=[VMEM],
        out_specs=VMEM,
        scratch_shapes=[
            pltpu.VMEM((peers, 1, D), F32),
            pltpu.VMEM((1, D), F32),
            pltpu.VMEM((regions, 1, D), F32),
            pltpu.VMEM((TAPS, 1, D), F32),
            pltpu.SemaphoreType.DMA((2 * peers + regions,)),
            pltpu.SemaphoreType.DMA((peers,)),
            pltpu.SemaphoreType.DMA((regions,)),
            pltpu.SemaphoreType.DMA((TAPS,)),
        ],
        compiler_params=params(collective_id=0, has_side_effects=True),
    )(terms)


def swap_rims(rims):
    count = lax.axis_size("grp")
    pairs = [(i, i + 1) for i in range(count - 1)]
    from_prev = lax.ppermute(rims[RIM:], "grp", pairs)
    from_next = lax.ppermute(rims[:RIM], "grp", [(b, a) for a, b in pairs])
    return from_prev, from_next


def on_device(features, cotangent, conv_weight, neighbours, halo_index, send_index, curve_slot):
    peers, slots = send_index.shape[1:]
    regions = lax.axis_size("grp")
    taps = neighbours.T
    send = send_index.reshape(1, peers * slots)
    curve = curve_slot.reshape(1, ROWS)
    lent = local(lend_kernel, shape((2 * RIM, D)), [], halo_index, features)
    from_prev, from_next = swap_rims(lent)
    padded = jnp.concatenate([features, from_prev, from_next], axis=0)
    outgoing = local(
        forward_kernel,
        shape((peers * slots, D)),
        [pltpu.VMEM((ROWS, D), F32)],
        taps,
        conv_weight,
        send,
        padded,
    )
    incoming = lax.all_to_all(outgoing, "pt", split_axis=0, concat_axis=0, tiled=True)
    filled = local(
        attention_kernel,
        shape((peers * slots, D)),
        [pltpu.VMEM((ROWS, D), BF16), pltpu.VMEM((ROWS, D), BF16)],
        curve,
        cotangent,
        incoming,
    )
    returned = lax.all_to_all(filled, "pt", split_axis=0, concat_axis=0, tiled=True)
    total, rims, terms = local(
        backward_kernel,
        (shape((ROWS, D), F32), shape((2 * RIM, D)), shape((TAPS, 1, D), F32)),
        [pltpu.VMEM((ROWS, D), BF16), pltpu.VMEM((TABLE, D), F32)],
        taps,
        conv_weight,
        send,
        padded,
        returned,
    )
    from_prev, from_next = swap_rims(rims)
    echoed = jnp.concatenate([from_prev, from_next], axis=0)
    grad_conv = total_terms(regions, peers, terms)
    grad_features = local(finish_kernel, shape((ROWS, D)), [], halo_index, total, echoed)
    return grad_features, grad_conv


def solution(mesh):
    in_specs = (
        P(("grp", "pt"), None),
        P(("grp", "pt"), None),
        P(),
        P(("grp", "pt"), None),
        P(("grp", "pt"), None),
        P(("grp", "pt"), None, None),
        P(("grp", "pt")),
    )
    out_specs = (P(("grp", "pt"), None), P())
    return jax.shard_map(
        on_device, mesh=mesh, in_specs=in_specs, out_specs=out_specs, check_vma=False
    )
```

```python
import functools

import jax
import jax.numpy as jnp
from jax import lax
from jax.experimental import pallas as pl
from jax.experimental.pallas import tpu as pltpu
from jax.sharding import PartitionSpec as P

D = 512
ROWS = 512
RIM = 64
TABLE = ROWS + 2 * RIM
TAPS = 27
CENTRE = TAPS // 2
HEAD_DIM = 16
LANES = 128
HALF = D // 2
BF16 = jnp.bfloat16
F32 = jnp.float32
I16 = jnp.int16
VMEM = pl.BlockSpec(memory_space=pltpu.VMEM)
MESH = pl.DeviceIdType.MESH


def dot(a, b, dims=((1,), (0,))):
    return lax.dot_general(a, b, (dims, ((), ())), preferred_element_type=F32)


def pick(mask):
    return jnp.where(mask, jnp.ones((), BF16), jnp.zeros((), BF16))


def rows_of(index_row, width):
    count = index_row.shape[1]
    column = jnp.broadcast_to(index_row, (LANES, count)).T.astype(I16)
    lane = lax.broadcasted_iota(jnp.int32, (count, LANES), 1).astype(I16)
    blocks = [pick(column == lane + jnp.asarray(start, I16)) for start in range(0, width, LANES)]
    return jnp.concatenate(blocks, axis=1)


def columns_of(index_row, height):
    count = index_row.shape[1]
    row = jnp.broadcast_to(index_row, (16, count)).astype(I16)
    sub = lax.broadcasted_iota(jnp.int32, (16, count), 0).astype(I16)
    blocks = [pick(row == sub + jnp.asarray(start, I16)) for start in range(0, height, 16)]
    return jnp.concatenate(blocks, axis=0)


def other_tap(step):
    return jnp.where(step < CENTRE, step, step + 1)


def each(first, last, act):
    def step(i, _):
        act(i)
        return 0

    lax.fori_loop(first, last, step, 0)


def head_grads(rows, cot):
    scaled = rows * jnp.asarray(HEAD_DIM**-0.5, BF16)
    head_of = lax.broadcasted_iota(jnp.int32, (ROWS, LANES), 1) // HEAD_DIM
    total = cot.astype(F32)
    for h in range(LANES // HEAD_DIM):
        inside = head_of == h
        keys = jnp.where(inside, rows, jnp.zeros((), BF16))
        scores = dot(keys, scaled, ((1,), (1,)))
        dprobs = dot(keys, cot, ((1,), (1,)))
        weights = jnp.exp(scores - jnp.max(scores, axis=0, keepdims=True))
        probs = weights * (1.0 / jnp.sum(weights, axis=0, keepdims=True))
        delta = jnp.sum(probs * dprobs, axis=0, keepdims=True)
        dscores = (probs * (dprobs - delta)).astype(BF16)
        grads = dot(probs.astype(BF16), cot) + dot(dscores, scaled)
        grads = grads + dot(dscores, scaled, ((0,), (0,)))
        total = total + jnp.where(inside, grads, 0.0)
    return total.astype(BF16)


def kernel(
    regions,
    peers,
    slots,
    taps_ref,
    weight_ref,
    send_ref,
    curve_ref,
    halo_ref,
    features_ref,
    cotangent_ref,
    out_ref,
    conv_ref,
    padded,
    lent,
    tap_rows,
    tap_columns,
    send_rows,
    send_columns,
    curve_rows,
    curve_columns,
    acc,
    outgoing,
    incoming,
    curve,
    grads,
    filled,
    returned,
    grad_hidden,
    spread,
    total,
    rims,
    echoed,
    terms,
    parts,
    part,
    sums,
    whole,
    halo_sems,
    echo_sems,
    out_sems,
    in_sems,
    filled_sems,
    returned_sems,
    term_sems,
    part_sems,
    sum_sems,
    whole_sems,
):
    grp = lax.axis_index("grp")
    me = lax.axis_index("pt")
    flat = peers * slots
    barrier = pltpu.get_barrier_semaphore()

    def greet_peer(step):
        peer = (me + step) % peers
        pl.semaphore_signal(barrier, inc=1, device_id=(grp, peer), device_id_type=MESH)

    def greet_region(step):
        other = (grp + step) % regions
        pl.semaphore_signal(barrier, inc=1, device_id=(other, me), device_id_type=MESH)

    each(1, peers, greet_peer)
    each(1, regions, greet_region)

    def rim_copies(source, target, sems, to_prev, to_next):
        prev = pltpu.make_async_remote_copy(
            src_ref=source.at[pl.ds(0, RIM)],
            dst_ref=target.at[pl.ds(to_prev, RIM)],
            send_sem=sems.at[0],
            recv_sem=sems.at[1],
            device_id=((grp + regions - 1) % regions, me),
            device_id_type=MESH,
        )
        next_ = pltpu.make_async_remote_copy(
            src_ref=source.at[pl.ds(RIM, RIM)],
            dst_ref=target.at[pl.ds(to_next, RIM)],
            send_sem=sems.at[2],
            recv_sem=sems.at[3],
            device_id=((grp + 1) % regions, me),
            device_id_type=MESH,
        )
        return prev, next_

    def start_rims(copies):
        pl.when(grp > 0)(copies[0].start)
        pl.when(grp < regions - 1)(copies[1].start)

    def take_rims(copies):
        pl.when(grp < regions - 1)(copies[0].wait_recv)
        pl.when(grp > 0)(copies[1].wait_recv)

    def end_rims(copies):
        pl.when(grp > 0)(copies[0].wait_send)
        pl.when(grp < regions - 1)(copies[1].wait_send)

    lent[...] = dot(rows_of(halo_ref[...], ROWS), features_ref[...]).astype(BF16)
    padded[:ROWS, :] = features_ref[...]

    @pl.when(grp == 0)
    def _():
        padded[ROWS : ROWS + RIM, :] = jnp.zeros((RIM, D), BF16)
        echoed[:RIM, :] = jnp.zeros((RIM, D), BF16)

    @pl.when(grp == regions - 1)
    def _():
        padded[ROWS + RIM :, :] = jnp.zeros((RIM, D), BF16)
        echoed[RIM:, :] = jnp.zeros((RIM, D), BF16)

    pl.semaphore_wait(barrier, peers - 1 + regions - 1)
    halo = rim_copies(lent, padded, halo_sems, ROWS + RIM, ROWS)
    start_rims(halo)

    def build_rows(step):
        k = other_tap(step)
        tap_rows[k] = rows_of(taps_ref[pl.ds(k, 1), :], TABLE)

    each(0, TAPS - 1, build_rows)
    send_rows[...] = rows_of(send_ref[...], ROWS)
    take_rims(halo)

    def send_block(source, target, send_sem, recv_sem, lanes):
        def one(step):
            peer = (me + step) % peers
            pltpu.make_async_remote_copy(
                src_ref=source.at[peer, :, lanes],
                dst_ref=target.at[me, :, lanes],
                send_sem=send_sem,
                recv_sem=recv_sem,
                device_id=(grp, peer),
                device_id_type=MESH,
            ).start()

        each(1, peers, one)
        target[me, :, lanes] = source[me, :, lanes]

    def wait_blocks(buffer, sem, lanes):
        view = buffer.at[pl.ds(0, peers - 1), :, lanes]
        pltpu.make_async_copy(view, view, sem).wait()

    everything = pl.ds(0, HALF)

    def forward(half):
        span = pl.ds(pl.multiple_of(half * HALF, HALF), HALF)
        own = padded[:ROWS, span].astype(F32)
        acc[...] = own + own * weight_ref[CENTRE : CENTRE + 1, span]

        def tap(step):
            k = other_tap(step)
            acc[...] += dot(tap_rows[k], padded[:, span]) * weight_ref[pl.ds(k, 1), span]

        each(0, TAPS - 1, tap)
        hidden = acc[...].astype(BF16)
        outgoing[half] = dot(send_rows[...], hidden).astype(BF16).reshape(peers, slots, HALF)
        send_block(outgoing.at[half], incoming.at[half], out_sems.at[half], in_sems.at[half], everything)

    each(0, 2, forward)

    def build_columns(step):
        k = other_tap(step)
        tap_columns[k] = columns_of(taps_ref[pl.ds(k, 1), :], TABLE)

    each(0, TAPS - 1, build_columns)
    curve_rows[...] = rows_of(curve_ref[...], flat)
    curve_columns[...] = columns_of(curve_ref[...], flat)
    send_columns[...] = columns_of(send_ref[...], ROWS)

    def attend(half):
        wait_blocks(incoming.at[half], in_sems.at[half], everything)
        curve[...] = dot(curve_rows[...], incoming[half].reshape(flat, HALF)).astype(BF16)

        def group(part_of):
            lanes = pl.ds(pl.multiple_of(part_of * LANES, LANES), LANES)
            span = pl.ds(pl.multiple_of(half * HALF + part_of * LANES, LANES), LANES)
            grads[...] = head_grads(curve[:, lanes], cotangent_ref[:, span])
            placed = dot(curve_columns[...], grads[...]).astype(BF16)
            filled[half, :, :, lanes] = placed.reshape(peers, slots, LANES)
            index = half * 2 + part_of
            send_block(
                filled.at[half], returned.at[half], filled_sems.at[index], returned_sems.at[index], lanes
            )

        each(0, 2, group)

    each(0, 2, attend)

    def backward(half):
        span = pl.ds(pl.multiple_of(half * HALF, HALF), HALF)
        for part_of in range(2):
            lanes = pl.ds(part_of * LANES, LANES)
            wait_blocks(returned.at[half], returned_sems.at[half * 2 + part_of], lanes)
        grad_hidden[...] = dot(send_columns[...], returned[half].reshape(flat, HALF)).astype(BF16)
        grad = grad_hidden[...].astype(F32)
        spread[:ROWS, :] = grad + grad * weight_ref[CENTRE : CENTRE + 1, span]
        spread[ROWS:, :] = jnp.zeros((2 * RIM, HALF), F32)
        terms[CENTRE, :, span] = jnp.sum(grad * padded[:ROWS, span].astype(F32), axis=0, keepdims=True)

        def tap(step):
            k = other_tap(step)
            landed = dot(tap_columns[k], grad_hidden[...])
            spread[...] += landed * weight_ref[pl.ds(k, 1), span]
            terms[k, :, span] = jnp.sum(landed * padded[:, span].astype(F32), axis=0, keepdims=True)

        each(0, TAPS - 1, tap)
        total[:, span] = spread[:ROWS, :]
        rims[:, span] = spread[ROWS:, :].astype(BF16)

    each(0, 2, backward)

    echo = rim_copies(rims, echoed, echo_sems, RIM, 0)
    start_rims(echo)

    def to_owner(step):
        peer = (me + step) % peers
        return peer, pltpu.make_async_remote_copy(
            src_ref=terms.at[peer % TAPS],
            dst_ref=parts.at[me],
            send_sem=term_sems.at[peer],
            recv_sem=part_sems.at[me],
            device_id=(grp, peer),
            device_id_type=MESH,
        )

    def from_peer(step):
        peer = (me + peers - step) % peers
        return pltpu.make_async_remote_copy(
            src_ref=terms.at[0],
            dst_ref=parts.at[peer],
            send_sem=term_sems.at[peer],
            recv_sem=part_sems.at[peer],
            device_id=(grp, peer),
            device_id_type=MESH,
        )

    def to_region(step):
        other = (grp + step) % regions
        return pltpu.make_async_remote_copy(
            src_ref=part,
            dst_ref=sums.at[grp],
            send_sem=term_sems.at[peers + other],
            recv_sem=sum_sems.at[grp],
            device_id=(other, me),
            device_id_type=MESH,
        )

    def from_region(step):
        other = (grp + regions - step) % regions
        return pltpu.make_async_remote_copy(
            src_ref=part,
            dst_ref=sums.at[other],
            send_sem=term_sems.at[peers + other],
            recv_sem=sum_sems.at[other],
            device_id=(other, me),
            device_id_type=MESH,
        )

    def to_all(step):
        peer = (me + step) % peers
        return pltpu.make_async_remote_copy(
            src_ref=whole.at[me],
            dst_ref=whole.at[me],
            send_sem=term_sems.at[peers + regions + peer],
            recv_sem=whole_sems.at[me],
            device_id=(grp, peer),
            device_id_type=MESH,
        )

    def from_owner(peer):
        return pltpu.make_async_remote_copy(
            src_ref=whole.at[peer],
            dst_ref=whole.at[peer],
            send_sem=term_sems.at[peers + regions + peer],
            recv_sem=whole_sems.at[peer],
            device_id=(grp, peer),
            device_id_type=MESH,
        )

    def start_term(step):
        peer, copy = to_owner(step)
        pl.when(peer < TAPS)(copy.start)

    each(1, peers, start_term)

    take_rims(echo)
    out_ref[...] = (total[...] + dot(columns_of(halo_ref[...], ROWS), echoed[...])).astype(BF16)

    @pl.when(me < TAPS)
    def _():
        parts[me] = terms[me]
        each(1, peers, lambda step: from_peer(step).wait_recv())
        mine = jnp.sum(parts[...], axis=0)
        part[...] = mine
        sums[grp] = mine
        each(1, regions, lambda step: to_region(step).start())
        each(1, regions, lambda step: from_region(step).wait_recv())
        whole[me] = jnp.sum(sums[...], axis=0)
        each(1, peers, lambda step: to_all(step).start())

    end_rims(halo)
    end_rims(echo)
    for half in range(2):
        wait_blocks(outgoing.at[half], out_sems.at[half], everything)
        for part_of in range(2):
            lanes = pl.ds(part_of * LANES, LANES)
            wait_blocks(filled.at[half], filled_sems.at[half * 2 + part_of], lanes)

    def take(owner):
        @pl.when(owner != me)
        def _():
            from_owner(owner).wait_recv()

    each(0, TAPS, take)

    def end_term(step):
        peer, copy = to_owner(step)
        pl.when(peer < TAPS)(copy.wait_send)

    each(1, peers, end_term)

    @pl.when(me < TAPS)
    def _():
        each(1, regions, lambda step: to_region(step).wait_send())
        each(1, peers, lambda step: to_all(step).wait_send())

    for k in range(TAPS):
        conv_ref[k : k + 1, :] = whole[k]


def on_device(features, cotangent, conv_weight, neighbours, halo_index, send_index, curve_slot):
    peers, slots = send_index.shape[1:]
    regions = lax.axis_size("grp")
    flat = peers * slots
    args = (
        neighbours.T,
        conv_weight,
        send_index.reshape(1, flat),
        curve_slot.reshape(1, ROWS),
        halo_index,
        features,
        cotangent,
    )
    blocks = pltpu.VMEM((2, peers, slots, HALF), BF16)
    dma = pltpu.SemaphoreType.DMA
    return pl.pallas_call(
        functools.partial(kernel, regions, peers, slots),
        out_shape=(
            jax.ShapeDtypeStruct((ROWS, D), BF16),
            jax.ShapeDtypeStruct((TAPS, D), F32),
        ),
        in_specs=[VMEM] * len(args),
        out_specs=(VMEM, VMEM),
        scratch_shapes=[
            pltpu.VMEM((TABLE, D), BF16),
            pltpu.VMEM((2 * RIM, D), BF16),
            pltpu.VMEM((TAPS, ROWS, TABLE), BF16),
            pltpu.VMEM((TAPS, TABLE, ROWS), BF16),
            pltpu.VMEM((flat, ROWS), BF16),
            pltpu.VMEM((ROWS, flat), BF16),
            pltpu.VMEM((ROWS, flat), BF16),
            pltpu.VMEM((flat, ROWS), BF16),
            pltpu.VMEM((ROWS, HALF), F32),
            blocks,
            blocks,
            pltpu.VMEM((ROWS, HALF), BF16),
            pltpu.VMEM((ROWS, LANES), BF16),
            blocks,
            blocks,
            pltpu.VMEM((ROWS, HALF), BF16),
            pltpu.VMEM((TABLE, HALF), F32),
            pltpu.VMEM((ROWS, D), F32),
            pltpu.VMEM((2 * RIM, D), BF16),
            pltpu.VMEM((2 * RIM, D), BF16),
            pltpu.VMEM((TAPS, 1, D), F32),
            pltpu.VMEM((peers, 1, D), F32),
            pltpu.VMEM((1, D), F32),
            pltpu.VMEM((regions, 1, D), F32),
            pltpu.VMEM((TAPS, 1, D), F32),
            dma((4,)),
            dma((4,)),
            dma((2,)),
            dma((2,)),
            dma((4,)),
            dma((4,)),
            dma((2 * peers + regions,)),
            dma((peers,)),
            dma((regions,)),
            dma((TAPS,)),
        ],
        compiler_params=pltpu.CompilerParams(
            vmem_limit_bytes=60 * 2**20, collective_id=0, has_side_effects=True
        ),
    )(*args)


def solution(mesh):
    in_specs = (
        P(("grp", "pt"), None),
        P(("grp", "pt"), None),
        P(),
        P(("grp", "pt"), None),
        P(("grp", "pt"), None),
        P(("grp", "pt"), None, None),
        P(("grp", "pt")),
    )
    out_specs = (P(("grp", "pt"), None), P())
    return jax.shard_map(
        on_device, mesh=mesh, in_specs=in_specs, out_specs=out_specs, check_vma=False
    )
```

```python
import functools

import jax
import jax.numpy as jnp
from jax import lax
from jax.experimental import pallas as pl
from jax.experimental.pallas import tpu as pltpu
from jax.sharding import PartitionSpec as P

D = 512
ROWS = 512
RIM = 64
TABLE = ROWS + 2 * RIM
TAPS = 27
CENTRE = TAPS // 2
HEAD_DIM = 16
LANES = 128
HALF = D // 2
BF16 = jnp.bfloat16
F32 = jnp.float32
I16 = jnp.int16
VMEM = pl.BlockSpec(memory_space=pltpu.VMEM)
MESH = pl.DeviceIdType.MESH


def dot(a, b, dims=((1,), (0,))):
    return lax.dot_general(a, b, (dims, ((), ())), preferred_element_type=F32)


def pick(mask):
    return jnp.where(mask, jnp.ones((), BF16), jnp.zeros((), BF16))


def rows_of(index_row, width):
    count = index_row.shape[1]
    column = jnp.broadcast_to(index_row, (LANES, count)).T.astype(I16)
    lane = lax.broadcasted_iota(jnp.int32, (count, LANES), 1).astype(I16)
    blocks = [pick(column == lane + jnp.asarray(start, I16)) for start in range(0, width, LANES)]
    return jnp.concatenate(blocks, axis=1)


def columns_of(index_row, height):
    count = index_row.shape[1]
    row = jnp.broadcast_to(index_row, (16, count)).astype(I16)
    sub = lax.broadcasted_iota(jnp.int32, (16, count), 0).astype(I16)
    blocks = [pick(row == sub + jnp.asarray(start, I16)) for start in range(0, height, 16)]
    return jnp.concatenate(blocks, axis=0)


def each(first, last, act):
    def step(i, _):
        act(i)
        return 0

    lax.fori_loop(first, last, step, 0)


def softmax_grads(scores, dprobs):
    weights = jnp.exp(scores - jnp.max(scores, axis=0, keepdims=True))
    inverse = 1.0 / jnp.sum(weights, axis=0, keepdims=True)
    delta = jnp.sum(weights * dprobs, axis=0, keepdims=True) * inverse
    probs = weights * inverse
    return probs.astype(BF16), (probs * (dprobs - delta)).astype(BF16)


def head_grads(rows, cot):
    scaled = rows * jnp.asarray(HEAD_DIM**-0.5, BF16)
    head_of = lax.broadcasted_iota(jnp.int32, (ROWS, LANES), 1) // HEAD_DIM
    heads = LANES // HEAD_DIM

    def products(h):
        keys = jnp.where(head_of == h, rows, jnp.zeros((), BF16))
        queries = [slice(start, start + LANES) for start in range(0, ROWS, LANES)]
        return [
            (dot(keys, scaled[at], ((1,), (1,))), dot(keys, cot[at], ((1,), (1,)))) for at in queries
        ]

    total = cot.astype(F32)
    ahead = products(0)
    for h in range(heads):
        now = ahead
        if h + 1 < heads:
            ahead = products(h + 1)
        pairs = [softmax_grads(*pair) for pair in now]
        probs = jnp.concatenate([pair[0] for pair in pairs], axis=1)
        dscores = jnp.concatenate([pair[1] for pair in pairs], axis=1)
        grads = dot(probs, cot) + dot(dscores, scaled) + dot(dscores, scaled, ((0,), (0,)))
        total = total + jnp.where(head_of == h, grads, 0.0)
    return total.astype(BF16)


def kernel(
    regions,
    peers,
    slots,
    taps_ref,
    weight_ref,
    send_ref,
    curve_ref,
    halo_ref,
    features_ref,
    cotangent_ref,
    out_ref,
    conv_ref,
    padded,
    lent,
    send_rows,
    send_columns,
    curve_rows,
    curve_columns,
    acc,
    outgoing,
    incoming,
    curve,
    grads,
    filled,
    returned,
    grad_hidden,
    spread,
    total,
    rims,
    echoed,
    terms,
    parts,
    part,
    sums,
    whole,
    halo_sems,
    echo_sems,
    out_sems,
    in_sems,
    filled_sems,
    returned_sems,
    part_sems,
    sum_sems,
    whole_sems,
):
    grp = lax.axis_index("grp")
    me = lax.axis_index("pt")
    flat = peers * slots
    share = parts.shape[1]
    send_row = jnp.concatenate([send_ref[p : p + 1, :] for p in range(peers)], axis=1)
    barrier = pltpu.get_barrier_semaphore()

    def greet_peer(step):
        peer = (me + step) % peers
        pl.semaphore_signal(barrier, inc=1, device_id=(grp, peer), device_id_type=MESH)

    def greet_region(step):
        other = (grp + step) % regions
        pl.semaphore_signal(barrier, inc=1, device_id=(other, me), device_id_type=MESH)

    each(1, peers, greet_peer)
    each(1, regions, greet_region)

    def rim_copies(source, target, sems, to_prev, to_next):
        prev = pltpu.make_async_remote_copy(
            src_ref=source.at[pl.ds(0, RIM)],
            dst_ref=target.at[pl.ds(to_prev, RIM)],
            send_sem=sems.at[0],
            recv_sem=sems.at[1],
            device_id=((grp + regions - 1) % regions, me),
            device_id_type=MESH,
        )
        next_ = pltpu.make_async_remote_copy(
            src_ref=source.at[pl.ds(RIM, RIM)],
            dst_ref=target.at[pl.ds(to_next, RIM)],
            send_sem=sems.at[2],
            recv_sem=sems.at[3],
            device_id=((grp + 1) % regions, me),
            device_id_type=MESH,
        )
        return prev, next_

    def start_rims(copies):
        pl.when(grp > 0)(copies[0].start)
        pl.when(grp < regions - 1)(copies[1].start)

    def take_rims(copies):
        pl.when(grp < regions - 1)(copies[0].wait_recv)
        pl.when(grp > 0)(copies[1].wait_recv)

    def end_rims(copies):
        pl.when(grp > 0)(copies[0].wait_send)
        pl.when(grp < regions - 1)(copies[1].wait_send)

    terms[TAPS:] = jnp.zeros((regions * share - TAPS, 1, D), F32)
    lent[...] = dot(rows_of(halo_ref[...], ROWS), features_ref[...]).astype(BF16)
    padded[:ROWS, :] = features_ref[...]

    @pl.when(grp == 0)
    def _():
        padded[ROWS : ROWS + RIM, :] = jnp.zeros((RIM, D), BF16)
        echoed[:RIM, :] = jnp.zeros((RIM, D), BF16)

    @pl.when(grp == regions - 1)
    def _():
        padded[ROWS + RIM :, :] = jnp.zeros((RIM, D), BF16)
        echoed[RIM:, :] = jnp.zeros((RIM, D), BF16)

    def weighted(step, half, one_hot, table):
        span = pl.ds(pl.multiple_of(half * HALF, HALF), HALF)
        added = jnp.zeros((ROWS, HALF), F32)
        for k in range(CENTRE):
            k = step * (CENTRE + 1) + k
            picked = dot(one_hot(taps_ref[pl.ds(k, 1), :]), table[:, span])
            added = added + picked * weight_ref[pl.ds(k, 1), span]
        return added

    def from_own(half):
        span = pl.ds(pl.multiple_of(half * HALF, HALF), HALF)
        own = padded[:ROWS, span].astype(F32)
        acc[half] = own + own * weight_ref[CENTRE : CENTRE + 1, span]

        def taps(step):
            acc[half] += weighted(step, half, lambda row: rows_of(row, ROWS), padded.at[pl.ds(0, ROWS)])

        each(0, 2, taps)

    each(0, 2, from_own)
    pl.semaphore_wait(barrier, peers - 1 + regions - 1)
    halo = rim_copies(lent, padded, halo_sems, ROWS + RIM, ROWS)
    start_rims(halo)
    send_rows[...] = rows_of(send_row, ROWS)
    send_columns[...] = columns_of(send_row, ROWS)
    curve_rows[...] = rows_of(curve_ref[...], flat)
    curve_columns[...] = columns_of(curve_ref[...], flat)
    take_rims(halo)

    def send_block(source, target, send_sem, recv_sem, lanes):
        def one(step):
            peer = (me + step) % peers
            pltpu.make_async_remote_copy(
                src_ref=source.at[peer, :, lanes],
                dst_ref=target.at[me, :, lanes],
                send_sem=send_sem,
                recv_sem=recv_sem,
                device_id=(grp, peer),
                device_id_type=MESH,
            ).start()

        each(1, peers, one)
        target[me, :, lanes] = source[me, :, lanes]

    def wait_blocks(buffer, sem, lanes):
        view = buffer.at[pl.ds(0, peers - 1), :, lanes]
        pltpu.make_async_copy(view, view, sem).wait()

    def forward(half):
        def taps(step):
            acc[half] += weighted(
                step, half, lambda row: rows_of(row - ROWS, 2 * RIM), padded.at[pl.ds(ROWS, 2 * RIM)]
            )

        each(0, 2, taps)
        hidden = acc[half].astype(BF16)
        outgoing[half] = dot(send_rows[...], hidden).astype(BF16).reshape(peers, slots, HALF)

        def group(part_of):
            lanes = pl.ds(pl.multiple_of(part_of * LANES, LANES), LANES)
            index = half * 2 + part_of
            send_block(outgoing.at[half], incoming.at[half], out_sems.at[index], in_sems.at[index], lanes)

        each(0, 2, group)

    each(0, 2, forward)

    def attend(index):
        half = index // 2
        lanes = pl.ds(pl.multiple_of(index % 2 * LANES, LANES), LANES)
        span = pl.ds(pl.multiple_of(index * LANES, LANES), LANES)
        wait_blocks(incoming.at[half], in_sems.at[index], lanes)
        rows = incoming[half, :, :, lanes].reshape(flat, LANES)
        curve[...] = dot(curve_rows[...], rows).astype(BF16)
        grads[...] = head_grads(curve[...], cotangent_ref[:, span])
        placed = dot(curve_columns[...], grads[...]).astype(BF16)
        filled[half, :, :, lanes] = placed.reshape(peers, slots, LANES)
        send_block(filled.at[half], returned.at[half], filled_sems.at[index], returned_sems.at[index], lanes)

    each(0, 4, attend)

    def backward(half):
        span = pl.ds(pl.multiple_of(half * HALF, HALF), HALF)
        for part_of in range(2):
            lanes = pl.ds(part_of * LANES, LANES)
            wait_blocks(returned.at[half], returned_sems.at[half * 2 + part_of], lanes)
        grad_hidden[...] = dot(send_columns[...], returned[half].reshape(flat, HALF)).astype(BF16)
        grad = grad_hidden[...].astype(F32)
        spread[:ROWS, :] = grad + grad * weight_ref[CENTRE : CENTRE + 1, span]
        spread[ROWS:, :] = jnp.zeros((2 * RIM, HALF), F32)
        terms[CENTRE, :, span] = jnp.sum(grad * padded[:ROWS, span].astype(F32), axis=0, keepdims=True)

        def taps(step):
            added = jnp.zeros((TABLE, HALF), F32)
            for k in range(CENTRE):
                k = step * (CENTRE + 1) + k
                landed = dot(columns_of(taps_ref[pl.ds(k, 1), :], TABLE), grad_hidden[...])
                terms[k, :, span] = jnp.sum(landed * padded[:, span].astype(F32), axis=0, keepdims=True)
                added = added + landed * weight_ref[pl.ds(k, 1), span]
            spread[...] += added

        each(0, 2, taps)
        total[:, span] = spread[:ROWS, :]
        rims[:, span] = spread[ROWS:, :].astype(BF16)

    each(0, 2, backward)

    echo = rim_copies(rims, echoed, echo_sems, RIM, 0)
    start_rims(echo)

    def over_regions(source, target, sems):
        def one(step):
            other = (grp + step) % regions
            pltpu.make_async_remote_copy(
                src_ref=source(other),
                dst_ref=target.at[grp],
                send_sem=sems.at[0],
                recv_sem=sems.at[1],
                device_id=(other, me),
                device_id_type=MESH,
            ).start()

        each(1, regions, one)

    def wait_rows(buffer, sem, count):
        view = buffer.at[pl.ds(0, count)]
        pltpu.make_async_copy(view, view, sem).wait()

    over_regions(lambda other: terms.at[pl.ds(other * share, share)], parts, part_sems)

    take_rims(echo)
    out_ref[...] = (total[...] + dot(columns_of(halo_ref[...], ROWS), echoed[...])).astype(BF16)

    parts[grp] = terms[pl.ds(grp * share, share)]
    wait_rows(parts, part_sems.at[1], regions - 1)
    mine = jnp.sum(parts[...], axis=0)
    part[...] = mine
    sums[me] = mine

    def to_peer(step):
        peer = (me + step) % peers
        pltpu.make_async_remote_copy(
            src_ref=part,
            dst_ref=sums.at[me],
            send_sem=sum_sems.at[0],
            recv_sem=sum_sems.at[1],
            device_id=(grp, peer),
            device_id_type=MESH,
        ).start()

    each(1, peers, to_peer)
    wait_rows(sums, sum_sems.at[1], peers - 1)
    whole[grp] = jnp.sum(sums[...], axis=0)
    over_regions(lambda other: whole.at[grp], whole, whole_sems)
    end_rims(halo)
    end_rims(echo)
    for half in range(2):
        for part_of in range(2):
            lanes = pl.ds(part_of * LANES, LANES)
            wait_blocks(outgoing.at[half], out_sems.at[half * 2 + part_of], lanes)
            wait_blocks(filled.at[half], filled_sems.at[half * 2 + part_of], lanes)
    wait_rows(parts, part_sems.at[0], regions - 1)
    wait_rows(sums, sum_sems.at[0], peers - 1)
    wait_rows(whole, whole_sems.at[0], regions - 1)
    wait_rows(whole, whole_sems.at[1], regions - 1)
    for k in range(TAPS):
        conv_ref[k : k + 1, :] = whole[k // share, k % share]


def hand_over(grad_ref, conv_ref, grad_out_ref, conv_out_ref):
    grad_out_ref[...] = grad_ref[...]
    conv_out_ref[...] = conv_ref[...]


def on_device(features, cotangent, conv_weight, neighbours, halo_index, send_index, curve_slot):
    peers, slots = send_index.shape[1:]
    regions = lax.axis_size("grp")
    flat = peers * slots
    share = -(-TAPS // regions)
    args = (
        neighbours.T,
        conv_weight,
        send_index.reshape(peers, slots),
        curve_slot.reshape(1, ROWS),
        halo_index,
        features,
        cotangent,
    )
    blocks = pltpu.VMEM((2, peers, slots, HALF), BF16)
    dma = pltpu.SemaphoreType.DMA
    results = pl.pallas_call(
        functools.partial(kernel, regions, peers, slots),
        out_shape=(
            jax.ShapeDtypeStruct((ROWS, D), BF16),
            jax.ShapeDtypeStruct((TAPS, D), F32),
        ),
        in_specs=[VMEM] * len(args),
        out_specs=(VMEM, VMEM),
        scratch_shapes=[
            pltpu.VMEM((TABLE, D), BF16),
            pltpu.VMEM((2 * RIM, D), BF16),
            pltpu.VMEM((flat, ROWS), BF16),
            pltpu.VMEM((ROWS, flat), BF16),
            pltpu.VMEM((ROWS, flat), BF16),
            pltpu.VMEM((flat, ROWS), BF16),
            pltpu.VMEM((2, ROWS, HALF), F32),
            blocks,
            blocks,
            pltpu.VMEM((ROWS, LANES), BF16),
            pltpu.VMEM((ROWS, LANES), BF16),
            blocks,
            blocks,
            pltpu.VMEM((ROWS, HALF), BF16),
            pltpu.VMEM((TABLE, HALF), F32),
            pltpu.VMEM((ROWS, D), F32),
            pltpu.VMEM((2 * RIM, D), BF16),
            pltpu.VMEM((2 * RIM, D), BF16),
            pltpu.VMEM((regions * share, 1, D), F32),
            pltpu.VMEM((regions, share, 1, D), F32),
            pltpu.VMEM((share, 1, D), F32),
            pltpu.VMEM((peers, share, 1, D), F32),
            pltpu.VMEM((regions, share, 1, D), F32),
            dma((4,)),
            dma((4,)),
            dma((4,)),
            dma((4,)),
            dma((4,)),
            dma((4,)),
            dma((2,)),
            dma((2,)),
            dma((2,)),
        ],
        compiler_params=pltpu.CompilerParams(
            vmem_limit_bytes=60 * 2**20, collective_id=0, has_side_effects=True
        ),
    )(*args)
    return pl.pallas_call(
        hand_over,
        out_shape=tuple(jax.ShapeDtypeStruct(a.shape, a.dtype) for a in results),
        in_specs=[VMEM, VMEM],
        out_specs=(VMEM, VMEM),
    )(*results)


def solution(mesh):
    in_specs = (
        P(("grp", "pt"), None),
        P(("grp", "pt"), None),
        P(),
        P(("grp", "pt"), None),
        P(("grp", "pt"), None),
        P(("grp", "pt"), None, None),
        P(("grp", "pt")),
    )
    out_specs = (P(("grp", "pt"), None), P())
    return jax.shard_map(
        on_device, mesh=mesh, in_specs=in_specs, out_specs=out_specs, check_vma=False
    )
```

```python
import functools

import jax
import jax.numpy as jnp
from jax import lax
from jax.experimental import pallas as pl
from jax.experimental.pallas import tpu as pltpu
from jax.sharding import PartitionSpec as P

D = 512
ROWS = 512
RIM = 64
TABLE = ROWS + 2 * RIM
TAPS = 27
CENTRE = TAPS // 2
HEAD_DIM = 16
LANES = 128
HALF = D // 2
BF16 = jnp.bfloat16
F32 = jnp.float32
I16 = jnp.int16
VMEM = pl.BlockSpec(memory_space=pltpu.VMEM)
MESH = pl.DeviceIdType.MESH


def dot(a, b, dims=((1,), (0,))):
    return lax.dot_general(a, b, (dims, ((), ())), preferred_element_type=F32)


def pick(mask):
    return jnp.where(mask, jnp.ones((), BF16), jnp.zeros((), BF16))


def rows_of(index_row, width):
    count = index_row.shape[1]
    column = jnp.broadcast_to(index_row, (LANES, count)).T.astype(I16)
    lane = lax.broadcasted_iota(jnp.int32, (count, LANES), 1).astype(I16)
    blocks = [pick(column == lane + jnp.asarray(start, I16)) for start in range(0, width, LANES)]
    return jnp.concatenate(blocks, axis=1)


def columns_of(index_row, height):
    count = index_row.shape[1]
    row = jnp.broadcast_to(index_row, (16, count)).astype(I16)
    sub = lax.broadcasted_iota(jnp.int32, (16, count), 0).astype(I16)
    blocks = [pick(row == sub + jnp.asarray(start, I16)) for start in range(0, height, 16)]
    return jnp.concatenate(blocks, axis=0)


def each(first, last, act):
    def step(i, _):
        act(i)
        return 0

    lax.fori_loop(first, last, step, 0)


def softmax_grads(scores, dprobs):
    weights = jnp.exp(scores - jnp.max(scores, axis=0, keepdims=True))
    inverse = 1.0 / jnp.sum(weights, axis=0, keepdims=True)
    delta = jnp.sum(weights * dprobs, axis=0, keepdims=True) * inverse
    probs = weights * inverse
    return probs.astype(BF16), (probs * (dprobs - delta)).astype(BF16)


def head_grads(rows, cot):
    scaled = rows * jnp.asarray(HEAD_DIM**-0.5, BF16)
    head_of = lax.broadcasted_iota(jnp.int32, (ROWS, LANES), 1) // HEAD_DIM
    heads = LANES // HEAD_DIM

    def products(h):
        keys = jnp.where(head_of == h, rows, jnp.zeros((), BF16))
        queries = [slice(start, start + LANES) for start in range(0, ROWS, LANES)]
        return [
            (dot(keys, scaled[at], ((1,), (1,))), dot(keys, cot[at], ((1,), (1,)))) for at in queries
        ]

    total = cot.astype(F32)
    ahead = products(0)
    for h in range(heads):
        now = ahead
        if h + 1 < heads:
            ahead = products(h + 1)
        pairs = [softmax_grads(*pair) for pair in now]
        probs = jnp.concatenate([pair[0] for pair in pairs], axis=1)
        dscores = jnp.concatenate([pair[1] for pair in pairs], axis=1)
        grads = dot(probs, cot) + dot(dscores, scaled) + dot(dscores, scaled, ((0,), (0,)))
        total = total + jnp.where(head_of == h, grads, 0.0)
    return total.astype(BF16)


def kernel(
    regions,
    peers,
    slots,
    taps_ref,
    weight_ref,
    send_ref,
    curve_ref,
    halo_ref,
    features_ref,
    cotangent_ref,
    out_ref,
    conv_ref,
    padded,
    lent,
    send_rows,
    send_columns,
    curve_rows,
    curve_columns,
    acc,
    picks,
    outgoing,
    incoming,
    curve,
    grads,
    filled,
    returned,
    grad_hidden,
    spread,
    total,
    rims,
    echoed,
    partial,
    terms,
    parts,
    part,
    sums,
    whole,
    halo_sems,
    echo_sems,
    out_sems,
    in_sems,
    filled_sems,
    returned_sems,
    part_sems,
    sum_sems,
    whole_sems,
):
    grp = lax.axis_index("grp")
    me = lax.axis_index("pt")
    flat = peers * slots
    share = parts.shape[1]
    send_row = jnp.concatenate([send_ref[p : p + 1, :] for p in range(peers)], axis=1)
    barrier = pltpu.get_barrier_semaphore()

    def greet_peer(step):
        peer = (me + step) % peers
        pl.semaphore_signal(barrier, inc=1, device_id=(grp, peer), device_id_type=MESH)

    def greet_region(step):
        other = (grp + step) % regions
        pl.semaphore_signal(barrier, inc=1, device_id=(other, me), device_id_type=MESH)

    each(1, peers, greet_peer)
    each(1, regions, greet_region)

    def rim_copies(source, target, sems, to_prev, to_next):
        prev = pltpu.make_async_remote_copy(
            src_ref=source.at[pl.ds(0, RIM)],
            dst_ref=target.at[pl.ds(to_prev, RIM)],
            send_sem=sems.at[0],
            recv_sem=sems.at[1],
            device_id=((grp + regions - 1) % regions, me),
            device_id_type=MESH,
        )
        next_ = pltpu.make_async_remote_copy(
            src_ref=source.at[pl.ds(RIM, RIM)],
            dst_ref=target.at[pl.ds(to_next, RIM)],
            send_sem=sems.at[2],
            recv_sem=sems.at[3],
            device_id=((grp + 1) % regions, me),
            device_id_type=MESH,
        )
        return prev, next_

    def start_rims(copies):
        pl.when(grp > 0)(copies[0].start)
        pl.when(grp < regions - 1)(copies[1].start)

    def take_rims(copies):
        pl.when(grp < regions - 1)(copies[0].wait_recv)
        pl.when(grp > 0)(copies[1].wait_recv)

    def end_rims(copies):
        pl.when(grp > 0)(copies[0].wait_send)
        pl.when(grp < regions - 1)(copies[1].wait_send)

    terms[TAPS:] = jnp.zeros((regions * share - TAPS, 1, D), F32)
    lent[...] = dot(rows_of(halo_ref[...], ROWS), features_ref[...]).astype(BF16)
    padded[:ROWS, :] = features_ref[...]

    @pl.when(grp == 0)
    def _():
        padded[ROWS : ROWS + RIM, :] = jnp.zeros((RIM, D), BF16)
        echoed[:RIM, :] = jnp.zeros((RIM, D), BF16)

    @pl.when(grp == regions - 1)
    def _():
        padded[ROWS + RIM :, :] = jnp.zeros((RIM, D), BF16)
        echoed[RIM:, :] = jnp.zeros((RIM, D), BF16)

    def weighted(step, half, one_hot, table, first):
        span = pl.ds(pl.multiple_of(half * HALF, HALF), HALF)
        added = jnp.zeros((ROWS, HALF), F32)
        for k in range(CENTRE):
            k = step * (CENTRE + 1) + k
            picked = dot(one_hot(taps_ref[pl.ds(k, 1), :]), table[:, span])
            added = added + picked * weight_ref[pl.ds(k, 1), span]
            for part_of in range(2):
                found = picked[:, part_of * LANES : (part_of + 1) * LANES].astype(BF16)
                at = half * 2 + part_of
                picks[at, k] = found if first else picks[at, k] + found
        return added

    def from_own(half):
        span = pl.ds(pl.multiple_of(half * HALF, HALF), HALF)
        own = padded[:ROWS, span].astype(F32)
        acc[half] = own + own * weight_ref[CENTRE : CENTRE + 1, span]

        def taps(step):
            acc[half] += weighted(step, half, lambda row: rows_of(row, ROWS), padded.at[pl.ds(0, ROWS)], True)

        each(0, 2, taps)

    from_own(0)
    pl.semaphore_wait(barrier, peers - 1 + regions - 1)
    halo = rim_copies(lent, padded, halo_sems, ROWS + RIM, ROWS)
    start_rims(halo)
    send_rows[...] = rows_of(send_row, ROWS)
    send_columns[...] = columns_of(send_row, ROWS)
    curve_rows[...] = rows_of(curve_ref[...], flat)
    curve_columns[...] = columns_of(curve_ref[...], flat)
    from_own(1)
    take_rims(halo)

    def send_block(source, target, send_sem, recv_sem, lanes):
        def one(step):
            peer = (me + step) % peers
            pltpu.make_async_remote_copy(
                src_ref=source.at[peer, :, lanes],
                dst_ref=target.at[me, :, lanes],
                send_sem=send_sem,
                recv_sem=recv_sem,
                device_id=(grp, peer),
                device_id_type=MESH,
            ).start()

        each(1, peers, one)
        target[me, :, lanes] = source[me, :, lanes]

    def wait_blocks(buffer, sem, lanes):
        view = buffer.at[pl.ds(0, peers - 1), :, lanes]
        pltpu.make_async_copy(view, view, sem).wait()

    def forward(half):
        def taps(step):
            acc[half] += weighted(
                step, half, lambda row: rows_of(row - ROWS, 2 * RIM), padded.at[pl.ds(ROWS, 2 * RIM)], False
            )

        each(0, 2, taps)
        hidden = acc[half].astype(BF16)
        outgoing[half] = dot(send_rows[...], hidden).astype(BF16).reshape(peers, slots, HALF)

        def group(part_of):
            lanes = pl.ds(pl.multiple_of(part_of * LANES, LANES), LANES)
            index = half * 2 + part_of
            send_block(outgoing.at[half], incoming.at[half], out_sems.at[index], in_sems.at[index], lanes)

        each(0, 2, group)

    each(0, 2, forward)

    def attend(index):
        half = index // 2
        lanes = pl.ds(pl.multiple_of(index % 2 * LANES, LANES), LANES)
        span = pl.ds(pl.multiple_of(index * LANES, LANES), LANES)
        wait_blocks(incoming.at[half], in_sems.at[index], lanes)
        rows = incoming[half, :, :, lanes].reshape(flat, LANES)
        curve[...] = dot(curve_rows[...], rows).astype(BF16)
        grads[...] = head_grads(curve[...], cotangent_ref[:, span])
        placed = dot(curve_columns[...], grads[...]).astype(BF16)
        filled[half, :, :, lanes] = placed.reshape(peers, slots, LANES)
        send_block(filled.at[half], returned.at[half], filled_sems.at[index], returned_sems.at[index], lanes)

    each(0, 4, attend)

    def over_regions(source, target, sems):
        def one(step):
            other = (grp + step) % regions
            pltpu.make_async_remote_copy(
                src_ref=source(other),
                dst_ref=target.at[grp],
                send_sem=sems.at[0],
                recv_sem=sems.at[1],
                device_id=(other, me),
                device_id_type=MESH,
            ).start()

        each(1, regions, one)

    def wait_rows(buffer, sem, count):
        view = buffer.at[pl.ds(0, count)]
        pltpu.make_async_copy(view, view, sem).wait()

    def scatter_terms():
        over_regions(lambda other: terms.at[pl.ds(other * share, share)], parts, part_sems)

    def exchange_parts():
        parts[grp] = terms[pl.ds(grp * share, share)]
        wait_rows(parts, part_sems.at[1], regions - 1)
        mine = jnp.sum(parts[...], axis=0)
        part[...] = mine
        sums[me] = mine

        def to_peer(step):
            peer = (me + step) % peers
            pltpu.make_async_remote_copy(
                src_ref=part,
                dst_ref=sums.at[me],
                send_sem=sum_sems.at[0],
                recv_sem=sum_sems.at[1],
                device_id=(grp, peer),
                device_id_type=MESH,
            ).start()

        each(1, peers, to_peer)

    def backward(half):
        span = pl.ds(pl.multiple_of(half * HALF, HALF), HALF)
        for part_of in range(2):
            lanes = pl.ds(part_of * LANES, LANES)
            wait_blocks(returned.at[half], returned_sems.at[half * 2 + part_of], lanes)
        grad_hidden[...] = dot(send_columns[...], returned[half].reshape(flat, HALF)).astype(BF16)
        partial[...] = jnp.zeros((TAPS, 8, HALF), F32)

        def sum_terms(block):
            rows = pl.ds(pl.multiple_of(block * RIM, RIM), RIM)
            for part_of in range(2):
                lanes = slice(part_of * LANES, (part_of + 1) * LANES)
                grad = grad_hidden[rows, lanes].astype(F32)
                for k in range(TAPS):
                    if k == CENTRE:
                        found = padded[rows, span][:, lanes]
                    else:
                        found = picks[half * 2 + part_of, k, rows, :]
                    product = (grad * found.astype(F32)).reshape(RIM // 8, 8, LANES)
                    partial[k, :, lanes] += jnp.sum(product, axis=0)

        each(0, ROWS // RIM, sum_terms)
        terms[:TAPS, :, span] = jnp.sum(partial[...], axis=1, keepdims=True)
        pl.when(half == 1)(scatter_terms)
        grad = grad_hidden[...].astype(F32)
        spread[:ROWS, :] = grad + grad * weight_ref[CENTRE : CENTRE + 1, span]
        spread[ROWS:, :] = jnp.zeros((2 * RIM, HALF), F32)

        def taps(step):
            pl.when((half == 1) & (step == 1))(exchange_parts)
            added = jnp.zeros((TABLE, HALF), F32)
            for k in range(CENTRE):
                k = step * (CENTRE + 1) + k
                landed = dot(columns_of(taps_ref[pl.ds(k, 1), :], TABLE), grad_hidden[...])
                added = added + landed * weight_ref[pl.ds(k, 1), span]
            spread[...] += added

        each(0, 2, taps)
        total[:, span] = spread[:ROWS, :]
        rims[:, span] = spread[ROWS:, :].astype(BF16)

    each(0, 2, backward)

    echo = rim_copies(rims, echoed, echo_sems, RIM, 0)
    start_rims(echo)

    take_rims(echo)
    out_ref[...] = (total[...] + dot(columns_of(halo_ref[...], ROWS), echoed[...])).astype(BF16)

    wait_rows(sums, sum_sems.at[1], peers - 1)
    whole[grp] = jnp.sum(sums[...], axis=0)
    over_regions(lambda other: whole.at[grp], whole, whole_sems)
    end_rims(halo)
    end_rims(echo)
    for half in range(2):
        for part_of in range(2):
            lanes = pl.ds(part_of * LANES, LANES)
            wait_blocks(outgoing.at[half], out_sems.at[half * 2 + part_of], lanes)
            wait_blocks(filled.at[half], filled_sems.at[half * 2 + part_of], lanes)
    wait_rows(parts, part_sems.at[0], regions - 1)
    wait_rows(sums, sum_sems.at[0], peers - 1)
    wait_rows(whole, whole_sems.at[0], regions - 1)
    wait_rows(whole, whole_sems.at[1], regions - 1)
    for k in range(TAPS):
        conv_ref[k : k + 1, :] = whole[k // share, k % share]


def hand_over(grad_ref, conv_ref, grad_out_ref, conv_out_ref):
    grad_out_ref[...] = grad_ref[...]
    conv_out_ref[...] = conv_ref[...]


def on_device(features, cotangent, conv_weight, neighbours, halo_index, send_index, curve_slot):
    peers, slots = send_index.shape[1:]
    regions = lax.axis_size("grp")
    flat = peers * slots
    share = -(-TAPS // regions)
    args = (
        neighbours.T,
        conv_weight,
        send_index.reshape(peers, slots),
        curve_slot.reshape(1, ROWS),
        halo_index,
        features,
        cotangent,
    )
    blocks = pltpu.VMEM((2, peers, slots, HALF), BF16)
    dma = pltpu.SemaphoreType.DMA
    results = pl.pallas_call(
        functools.partial(kernel, regions, peers, slots),
        out_shape=(
            jax.ShapeDtypeStruct((ROWS, D), BF16),
            jax.ShapeDtypeStruct((TAPS, D), F32),
        ),
        in_specs=[VMEM] * len(args),
        out_specs=(VMEM, VMEM),
        scratch_shapes=[
            pltpu.VMEM((TABLE, D), BF16),
            pltpu.VMEM((2 * RIM, D), BF16),
            pltpu.VMEM((flat, ROWS), BF16),
            pltpu.VMEM((ROWS, flat), BF16),
            pltpu.VMEM((ROWS, flat), BF16),
            pltpu.VMEM((flat, ROWS), BF16),
            pltpu.VMEM((2, ROWS, HALF), F32),
            pltpu.VMEM((4, TAPS, ROWS, LANES), BF16),
            blocks,
            blocks,
            pltpu.VMEM((ROWS, LANES), BF16),
            pltpu.VMEM((ROWS, LANES), BF16),
            blocks,
            blocks,
            pltpu.VMEM((ROWS, HALF), BF16),
            pltpu.VMEM((TABLE, HALF), F32),
            pltpu.VMEM((ROWS, D), F32),
            pltpu.VMEM((2 * RIM, D), BF16),
            pltpu.VMEM((2 * RIM, D), BF16),
            pltpu.VMEM((TAPS, 8, HALF), F32),
            pltpu.VMEM((regions * share, 1, D), F32),
            pltpu.VMEM((regions, share, 1, D), F32),
            pltpu.VMEM((share, 1, D), F32),
            pltpu.VMEM((peers, share, 1, D), F32),
            pltpu.VMEM((regions, share, 1, D), F32),
            dma((4,)),
            dma((4,)),
            dma((4,)),
            dma((4,)),
            dma((4,)),
            dma((4,)),
            dma((2,)),
            dma((2,)),
            dma((2,)),
        ],
        compiler_params=pltpu.CompilerParams(
            vmem_limit_bytes=60 * 2**20, collective_id=0, has_side_effects=True
        ),
    )(*args)
    return pl.pallas_call(
        hand_over,
        out_shape=tuple(jax.ShapeDtypeStruct(a.shape, a.dtype) for a in results),
        in_specs=[VMEM, VMEM],
        out_specs=(VMEM, VMEM),
    )(*results)


def solution(mesh):
    in_specs = (
        P(("grp", "pt"), None),
        P(("grp", "pt"), None),
        P(),
        P(("grp", "pt"), None),
        P(("grp", "pt"), None),
        P(("grp", "pt"), None, None),
        P(("grp", "pt")),
    )
    out_specs = (P(("grp", "pt"), None), P())
    return jax.shard_map(
        on_device, mesh=mesh, in_specs=in_specs, out_specs=out_specs, check_vma=False
    )
```

```python
import functools

import jax
import jax.numpy as jnp
from jax import lax
from jax.experimental import pallas as pl
from jax.experimental.pallas import tpu as pltpu
from jax.sharding import PartitionSpec as P

D = 512
ROWS = 512
RIM = 64
TABLE = ROWS + 2 * RIM
TAPS = 27
CENTRE = TAPS // 2
HEAD_DIM = 16
LANES = 128
HALF = D // 2
BF16 = jnp.bfloat16
F32 = jnp.float32
I16 = jnp.int16
VMEM = pl.BlockSpec(memory_space=pltpu.VMEM)
MESH = pl.DeviceIdType.MESH


def dot(a, b, dims=((1,), (0,))):
    return lax.dot_general(a, b, (dims, ((), ())), preferred_element_type=F32)


def pick(mask):
    return jnp.where(mask, jnp.ones((), BF16), jnp.zeros((), BF16))


def rows_of(index_row, width):
    count = index_row.shape[1]
    column = jnp.broadcast_to(index_row, (LANES, count)).T.astype(I16)
    lane = lax.broadcasted_iota(jnp.int32, (count, LANES), 1).astype(I16)
    blocks = [pick(column == lane + jnp.asarray(start, I16)) for start in range(0, width, LANES)]
    return jnp.concatenate(blocks, axis=1)


def columns_of(index_row, height):
    count = index_row.shape[1]
    row = jnp.broadcast_to(index_row, (16, count)).astype(I16)
    sub = lax.broadcasted_iota(jnp.int32, (16, count), 0).astype(I16)
    blocks = [pick(row == sub + jnp.asarray(start, I16)) for start in range(0, height, 16)]
    return jnp.concatenate(blocks, axis=0)


def each(first, last, act):
    def step(i, _):
        act(i)
        return 0

    lax.fori_loop(first, last, step, 0)


def softmax_grads(scores, dprobs):
    weights = jnp.exp(scores - jnp.max(scores, axis=0, keepdims=True))
    inverse = 1.0 / jnp.sum(weights, axis=0, keepdims=True)
    delta = jnp.sum(weights * dprobs, axis=0, keepdims=True) * inverse
    probs = weights * inverse
    return probs.astype(BF16), (probs * (dprobs - delta)).astype(BF16)


def head_grads(rows, cot):
    scaled = rows * jnp.asarray(HEAD_DIM**-0.5, BF16)
    head_of = lax.broadcasted_iota(jnp.int32, (ROWS, LANES), 1) // HEAD_DIM
    heads = LANES // HEAD_DIM

    def products(h):
        keys = jnp.where(head_of == h, rows, jnp.zeros((), BF16))
        queries = [slice(start, start + LANES) for start in range(0, ROWS, LANES)]
        return [
            (dot(keys, scaled[at], ((1,), (1,))), dot(keys, cot[at], ((1,), (1,)))) for at in queries
        ]

    total = cot.astype(F32)
    ahead = products(0)
    for h in range(heads):
        now = ahead
        if h + 1 < heads:
            ahead = products(h + 1)
        pairs = [softmax_grads(*pair) for pair in now]
        probs = jnp.concatenate([pair[0] for pair in pairs], axis=1)
        dscores = jnp.concatenate([pair[1] for pair in pairs], axis=1)
        grads = dot(probs, cot) + dot(dscores, scaled) + dot(dscores, scaled, ((0,), (0,)))
        total = total + jnp.where(head_of == h, grads, 0.0)
    return total.astype(BF16)


def kernel(
    regions,
    peers,
    slots,
    taps_ref,
    weight_ref,
    send_ref,
    curve_ref,
    halo_ref,
    features_ref,
    cotangent_ref,
    out_ref,
    conv_ref,
    padded,
    lent,
    send_rows,
    send_columns,
    curve_rows,
    curve_columns,
    acc,
    picks,
    outgoing,
    incoming,
    curve,
    grads,
    filled,
    returned,
    grad_hidden,
    spread,
    total,
    rims,
    echoed,
    partial,
    terms,
    parts,
    part,
    sums,
    whole,
    halo_sems,
    echo_sems,
    out_sems,
    in_sems,
    filled_sems,
    returned_sems,
    part_sems,
    sum_sems,
    whole_sems,
):
    grp = lax.axis_index("grp")
    me = lax.axis_index("pt")
    flat = peers * slots
    share = parts.shape[1]
    send_row = jnp.concatenate([send_ref[p : p + 1, :] for p in range(peers)], axis=1)
    barrier = pltpu.get_barrier_semaphore()

    def greet_peer(step):
        peer = (me + step) % peers
        pl.semaphore_signal(barrier, inc=1, device_id=(grp, peer), device_id_type=MESH)

    def greet_region(step):
        other = (grp + step) % regions
        pl.semaphore_signal(barrier, inc=1, device_id=(other, me), device_id_type=MESH)

    each(1, peers, greet_peer)
    each(1, regions, greet_region)

    def rim_copies(source, target, sems, to_prev, to_next):
        prev = pltpu.make_async_remote_copy(
            src_ref=source.at[pl.ds(0, RIM)],
            dst_ref=target.at[pl.ds(to_prev, RIM)],
            send_sem=sems.at[0],
            recv_sem=sems.at[1],
            device_id=((grp + regions - 1) % regions, me),
            device_id_type=MESH,
        )
        next_ = pltpu.make_async_remote_copy(
            src_ref=source.at[pl.ds(RIM, RIM)],
            dst_ref=target.at[pl.ds(to_next, RIM)],
            send_sem=sems.at[2],
            recv_sem=sems.at[3],
            device_id=((grp + 1) % regions, me),
            device_id_type=MESH,
        )
        return prev, next_

    def start_rims(copies):
        pl.when(grp > 0)(copies[0].start)
        pl.when(grp < regions - 1)(copies[1].start)

    def take_rims(copies):
        pl.when(grp < regions - 1)(copies[0].wait_recv)
        pl.when(grp > 0)(copies[1].wait_recv)

    def end_rims(copies):
        pl.when(grp > 0)(copies[0].wait_send)
        pl.when(grp < regions - 1)(copies[1].wait_send)

    terms[TAPS:] = jnp.zeros((regions * share - TAPS, 1, D), F32)
    lent[...] = dot(rows_of(halo_ref[...], ROWS), features_ref[...]).astype(BF16)
    padded[:ROWS, :] = features_ref[...]

    @pl.when(grp == 0)
    def _():
        padded[ROWS : ROWS + RIM, :] = jnp.zeros((RIM, D), BF16)
        echoed[:RIM, :] = jnp.zeros((RIM, D), BF16)

    @pl.when(grp == regions - 1)
    def _():
        padded[ROWS + RIM :, :] = jnp.zeros((RIM, D), BF16)
        echoed[RIM:, :] = jnp.zeros((RIM, D), BF16)

    def weighted(step, half, one_hot, table, first):
        span = pl.ds(pl.multiple_of(half * HALF, HALF), HALF)
        added = jnp.zeros((ROWS, HALF), F32)
        for k in range(CENTRE):
            k = step * (CENTRE + 1) + k
            picked = dot(one_hot(taps_ref[pl.ds(k, 1), :]), table[:, span])
            added = added + picked * weight_ref[pl.ds(k, 1), span]
            for part_of in range(2):
                found = picked[:, part_of * LANES : (part_of + 1) * LANES].astype(BF16)
                at = half * 2 + part_of
                picks[at, k] = found if first else picks[at, k] + found
        return added

    def from_own(half):
        span = pl.ds(pl.multiple_of(half * HALF, HALF), HALF)
        own = padded[:ROWS, span].astype(F32)
        acc[half] = own + own * weight_ref[CENTRE : CENTRE + 1, span]

        def taps(step):
            acc[half] += weighted(step, half, lambda row: rows_of(row, ROWS), padded.at[pl.ds(0, ROWS)], True)

        each(0, 2, taps)

    from_own(0)
    pl.semaphore_wait(barrier, peers - 1 + regions - 1)
    halo = rim_copies(lent, padded, halo_sems, ROWS + RIM, ROWS)
    start_rims(halo)
    send_rows[...] = rows_of(send_row, ROWS)
    send_columns[...] = columns_of(send_row, ROWS)
    curve_rows[...] = rows_of(curve_ref[...], flat)
    curve_columns[...] = columns_of(curve_ref[...], flat)
    from_own(1)
    take_rims(halo)

    def send_block(source, target, send_sem, recv_sem, lanes):
        def one(step):
            peer = (me + step) % peers
            pltpu.make_async_remote_copy(
                src_ref=source.at[peer, :, lanes],
                dst_ref=target.at[me, :, lanes],
                send_sem=send_sem,
                recv_sem=recv_sem,
                device_id=(grp, peer),
                device_id_type=MESH,
            ).start()

        each(1, peers, one)
        target[me, :, lanes] = source[me, :, lanes]

    def wait_blocks(buffer, sem, lanes):
        view = buffer.at[pl.ds(0, peers - 1), :, lanes]
        pltpu.make_async_copy(view, view, sem).wait()

    def forward(half):
        def taps(step):
            acc[half] += weighted(
                step, half, lambda row: rows_of(row - ROWS, 2 * RIM), padded.at[pl.ds(ROWS, 2 * RIM)], False
            )

        each(0, 2, taps)
        hidden = acc[half].astype(BF16)
        outgoing[half] = dot(send_rows[...], hidden).astype(BF16).reshape(peers, slots, HALF)

        def group(part_of):
            lanes = pl.ds(pl.multiple_of(part_of * LANES, LANES), LANES)
            index = half * 2 + part_of
            send_block(outgoing.at[half], incoming.at[half], out_sems.at[index], in_sems.at[index], lanes)

        each(0, 2, group)

    each(0, 2, forward)

    def attend(index):
        half = index // 2
        lanes = pl.ds(pl.multiple_of(index % 2 * LANES, LANES), LANES)
        span = pl.ds(pl.multiple_of(index * LANES, LANES), LANES)
        wait_blocks(incoming.at[half], in_sems.at[index], lanes)
        rows = incoming[half, :, :, lanes].reshape(flat, LANES)
        curve[...] = dot(curve_rows[...], rows).astype(BF16)
        grads[...] = head_grads(curve[...], cotangent_ref[:, span])
        placed = dot(curve_columns[...], grads[...]).astype(BF16)
        filled[half, :, :, lanes] = placed.reshape(peers, slots, LANES)
        send_block(filled.at[half], returned.at[half], filled_sems.at[index], returned_sems.at[index], lanes)

    each(0, 4, attend)

    def over_regions(source, target, sems):
        def one(step):
            other = (grp + step) % regions
            pltpu.make_async_remote_copy(
                src_ref=source(other),
                dst_ref=target.at[grp],
                send_sem=sems.at[0],
                recv_sem=sems.at[1],
                device_id=(other, me),
                device_id_type=MESH,
            ).start()

        each(1, regions, one)

    def wait_rows(buffer, sem, count):
        view = buffer.at[pl.ds(0, count)]
        pltpu.make_async_copy(view, view, sem).wait()

    def scatter_terms():
        over_regions(lambda other: terms.at[pl.ds(other * share, share)], parts, part_sems)

    def exchange_parts():
        parts[grp] = terms[pl.ds(grp * share, share)]
        wait_rows(parts, part_sems.at[1], regions - 1)
        mine = jnp.sum(parts[...], axis=0)
        part[...] = mine
        sums[me] = mine

        def to_peer(step):
            peer = (me + step) % peers
            pltpu.make_async_remote_copy(
                src_ref=part,
                dst_ref=sums.at[me],
                send_sem=sum_sems.at[0],
                recv_sem=sum_sems.at[1],
                device_id=(grp, peer),
                device_id_type=MESH,
            ).start()

        each(1, peers, to_peer)

    def finish_sums():
        wait_rows(sums, sum_sems.at[1], peers - 1)
        whole[grp] = jnp.sum(sums[...], axis=0)
        over_regions(lambda other: whole.at[grp], whole, whole_sems)

    def collect(index):
        half = index // 2
        lanes = pl.ds(pl.multiple_of(index % 2 * LANES, LANES), LANES)
        span = pl.ds(pl.multiple_of(index * LANES, LANES), LANES)
        wait_blocks(returned.at[half], returned_sems.at[index], lanes)
        rows = returned[half, :, :, lanes].reshape(flat, LANES)
        grad_hidden[:, span] = dot(send_columns[...], rows).astype(BF16)
        partial[...] = jnp.zeros((TAPS, 8, LANES), F32)

        def sum_terms(block):
            rows = pl.ds(pl.multiple_of(block * RIM, RIM), RIM)
            grad = grad_hidden[rows, span].astype(F32)
            for k in range(TAPS):
                found = padded[rows, span] if k == CENTRE else picks[index, k, rows, :]
                product = (grad * found.astype(F32)).reshape(RIM // 8, 8, LANES)
                partial[k] += jnp.sum(product, axis=0)

        each(0, ROWS // RIM, sum_terms)
        terms[:TAPS, :, span] = jnp.sum(partial[...], axis=1, keepdims=True)

    def end_terms():
        collect(3)
        scatter_terms()

    each(0, 3, collect)

    def backward(half):
        span = pl.ds(pl.multiple_of(half * HALF, HALF), HALF)
        grad = grad_hidden[:, span].astype(F32)
        spread[:ROWS, :] = grad + grad * weight_ref[CENTRE : CENTRE + 1, span]
        spread[ROWS:, :] = jnp.zeros((2 * RIM, HALF), F32)

        def taps(step):
            pl.when((half == 0) & (step == 1))(end_terms)
            pl.when((half == 1) & (step == 0))(exchange_parts)
            added = jnp.zeros((TABLE, HALF), F32)
            for k in range(CENTRE):
                k = step * (CENTRE + 1) + k
                landed = dot(columns_of(taps_ref[pl.ds(k, 1), :], TABLE), grad_hidden[:, span])
                added = added + landed * weight_ref[pl.ds(k, 1), span]
            spread[...] += added

        each(0, 2, taps)
        total[:, span] = spread[:ROWS, :]
        rims[:, span] = spread[ROWS:, :].astype(BF16)

    each(0, 2, backward)

    echo = rim_copies(rims, echoed, echo_sems, RIM, 0)
    start_rims(echo)
    finish_sums()
    take_rims(echo)
    out_ref[...] = (total[...] + dot(columns_of(halo_ref[...], ROWS), echoed[...])).astype(BF16)

    end_rims(halo)
    end_rims(echo)
    for half in range(2):
        for part_of in range(2):
            lanes = pl.ds(part_of * LANES, LANES)
            wait_blocks(outgoing.at[half], out_sems.at[half * 2 + part_of], lanes)
            wait_blocks(filled.at[half], filled_sems.at[half * 2 + part_of], lanes)
    wait_rows(parts, part_sems.at[0], regions - 1)
    wait_rows(sums, sum_sems.at[0], peers - 1)
    wait_rows(whole, whole_sems.at[0], regions - 1)
    wait_rows(whole, whole_sems.at[1], regions - 1)
    for k in range(TAPS):
        conv_ref[k : k + 1, :] = whole[k // share, k % share]


def hand_over(grad_ref, conv_ref, grad_out_ref, conv_out_ref):
    grad_out_ref[...] = grad_ref[...]
    conv_out_ref[...] = conv_ref[...]


def on_device(features, cotangent, conv_weight, neighbours, halo_index, send_index, curve_slot):
    peers, slots = send_index.shape[1:]
    regions = lax.axis_size("grp")
    flat = peers * slots
    share = -(-TAPS // regions)
    args = (
        neighbours.T,
        conv_weight,
        send_index.reshape(peers, slots),
        curve_slot.reshape(1, ROWS),
        halo_index,
        features,
        cotangent,
    )
    blocks = pltpu.VMEM((2, peers, slots, HALF), BF16)
    dma = pltpu.SemaphoreType.DMA
    results = pl.pallas_call(
        functools.partial(kernel, regions, peers, slots),
        out_shape=(
            jax.ShapeDtypeStruct((ROWS, D), BF16),
            jax.ShapeDtypeStruct((TAPS, D), F32),
        ),
        in_specs=[VMEM] * len(args),
        out_specs=(VMEM, VMEM),
        scratch_shapes=[
            pltpu.VMEM((TABLE, D), BF16),
            pltpu.VMEM((2 * RIM, D), BF16),
            pltpu.VMEM((flat, ROWS), BF16),
            pltpu.VMEM((ROWS, flat), BF16),
            pltpu.VMEM((ROWS, flat), BF16),
            pltpu.VMEM((flat, ROWS), BF16),
            pltpu.VMEM((2, ROWS, HALF), F32),
            pltpu.VMEM((4, TAPS, ROWS, LANES), BF16),
            blocks,
            blocks,
            pltpu.VMEM((ROWS, LANES), BF16),
            pltpu.VMEM((ROWS, LANES), BF16),
            blocks,
            blocks,
            pltpu.VMEM((ROWS, D), BF16),
            pltpu.VMEM((TABLE, HALF), F32),
            pltpu.VMEM((ROWS, D), F32),
            pltpu.VMEM((2 * RIM, D), BF16),
            pltpu.VMEM((2 * RIM, D), BF16),
            pltpu.VMEM((TAPS, 8, LANES), F32),
            pltpu.VMEM((regions * share, 1, D), F32),
            pltpu.VMEM((regions, share, 1, D), F32),
            pltpu.VMEM((share, 1, D), F32),
            pltpu.VMEM((peers, share, 1, D), F32),
            pltpu.VMEM((regions, share, 1, D), F32),
            dma((4,)),
            dma((4,)),
            dma((4,)),
            dma((4,)),
            dma((4,)),
            dma((4,)),
            dma((2,)),
            dma((2,)),
            dma((2,)),
        ],
        compiler_params=pltpu.CompilerParams(
            vmem_limit_bytes=60 * 2**20, collective_id=0, has_side_effects=True
        ),
    )(*args)
    return pl.pallas_call(
        hand_over,
        out_shape=tuple(jax.ShapeDtypeStruct(a.shape, a.dtype) for a in results),
        in_specs=[VMEM, VMEM],
        out_specs=(VMEM, VMEM),
    )(*results)


def solution(mesh):
    in_specs = (
        P(("grp", "pt"), None),
        P(("grp", "pt"), None),
        P(),
        P(("grp", "pt"), None),
        P(("grp", "pt"), None),
        P(("grp", "pt"), None, None),
        P(("grp", "pt")),
    )
    out_specs = (P(("grp", "pt"), None), P())
    return jax.shard_map(
        on_device, mesh=mesh, in_specs=in_specs, out_specs=out_specs, check_vma=False
    )
```

```python
import functools

import jax
import jax.numpy as jnp
from jax import lax
from jax.experimental import pallas as pl
from jax.experimental.pallas import tpu as pltpu
from jax.sharding import PartitionSpec as P

D = 512
ROWS = 512
RIM = 64
TABLE = ROWS + 2 * RIM
TAPS = 27
CENTRE = TAPS // 2
HEAD_DIM = 16
LANES = 128
HALF = D // 2
BF16 = jnp.bfloat16
F32 = jnp.float32
I16 = jnp.int16
VMEM = pl.BlockSpec(memory_space=pltpu.VMEM)
MESH = pl.DeviceIdType.MESH


def dot(a, b, dims=((1,), (0,))):
    return lax.dot_general(a, b, (dims, ((), ())), preferred_element_type=F32)


def pick(mask):
    return jnp.where(mask, jnp.ones((), BF16), jnp.zeros((), BF16))


def rows_of(index_row, width):
    count = index_row.shape[1]
    column = jnp.broadcast_to(index_row, (LANES, count)).T.astype(I16)
    lane = lax.broadcasted_iota(jnp.int32, (count, LANES), 1).astype(I16)
    blocks = [pick(column == lane + jnp.asarray(start, I16)) for start in range(0, width, LANES)]
    return jnp.concatenate(blocks, axis=1)


def columns_of(index_row, height):
    count = index_row.shape[1]
    row = jnp.broadcast_to(index_row, (16, count)).astype(I16)
    sub = lax.broadcasted_iota(jnp.int32, (16, count), 0).astype(I16)
    blocks = [pick(row == sub + jnp.asarray(start, I16)) for start in range(0, height, 16)]
    return jnp.concatenate(blocks, axis=0)


def each(first, last, act):
    def step(i, _):
        act(i)
        return 0

    lax.fori_loop(first, last, step, 0)


def softmax_grads(scores, dprobs):
    weights = jnp.exp(scores - jnp.max(scores, axis=0, keepdims=True))
    inverse = 1.0 / jnp.sum(weights, axis=0, keepdims=True)
    delta = jnp.sum(weights * dprobs, axis=0, keepdims=True) * inverse
    probs = weights * inverse
    return probs.astype(BF16), (probs * (dprobs - delta)).astype(BF16)


def head_grads(rows, cot):
    scaled = rows * jnp.asarray(HEAD_DIM**-0.5, BF16)
    head_of = lax.broadcasted_iota(jnp.int32, (ROWS, LANES), 1) // HEAD_DIM
    heads = LANES // HEAD_DIM

    def products(h):
        keys = jnp.where(head_of == h, rows, jnp.zeros((), BF16))
        queries = [slice(start, start + LANES) for start in range(0, ROWS, LANES)]
        return [
            (dot(keys, scaled[at], ((1,), (1,))), dot(keys, cot[at], ((1,), (1,)))) for at in queries
        ]

    total = cot.astype(F32)
    ahead = products(0)
    for h in range(heads):
        now = ahead
        if h + 1 < heads:
            ahead = products(h + 1)
        pairs = [softmax_grads(*pair) for pair in now]
        probs = jnp.concatenate([pair[0] for pair in pairs], axis=1)
        dscores = jnp.concatenate([pair[1] for pair in pairs], axis=1)
        grads = dot(probs, cot) + dot(dscores, scaled) + dot(dscores, scaled, ((0,), (0,)))
        total = total + jnp.where(head_of == h, grads, 0.0)
    return total.astype(BF16)


def kernel(
    regions,
    peers,
    slots,
    taps_ref,
    weight_ref,
    send_ref,
    curve_ref,
    halo_ref,
    features_ref,
    cotangent_ref,
    out_ref,
    conv_ref,
    padded,
    lent,
    send_rows,
    send_columns,
    curve_rows,
    curve_columns,
    acc,
    picks,
    outgoing,
    incoming,
    curve,
    grads,
    filled,
    returned,
    grad_hidden,
    spread,
    total,
    rims,
    echoed,
    partial,
    terms,
    parts,
    part,
    sums,
    whole,
    halo_sems,
    echo_sems,
    out_sems,
    in_sems,
    filled_sems,
    returned_sems,
    part_sems,
    sum_sems,
    whole_sems,
):
    grp = lax.axis_index("grp")
    me = lax.axis_index("pt")
    flat = peers * slots
    share = parts.shape[1]
    send_row = jnp.concatenate([send_ref[p : p + 1, :] for p in range(peers)], axis=1)
    barrier = pltpu.get_barrier_semaphore()

    def greet_peer(step):
        peer = (me + step) % peers
        pl.semaphore_signal(barrier, inc=1, device_id=(grp, peer), device_id_type=MESH)

    def greet_region(step):
        other = (grp + step) % regions
        pl.semaphore_signal(barrier, inc=1, device_id=(other, me), device_id_type=MESH)

    each(1, peers, greet_peer)
    each(1, regions, greet_region)

    def rim_copies(source, target, sems, to_prev, to_next):
        prev = pltpu.make_async_remote_copy(
            src_ref=source.at[pl.ds(0, RIM)],
            dst_ref=target.at[pl.ds(to_prev, RIM)],
            send_sem=sems.at[0],
            recv_sem=sems.at[1],
            device_id=((grp + regions - 1) % regions, me),
            device_id_type=MESH,
        )
        next_ = pltpu.make_async_remote_copy(
            src_ref=source.at[pl.ds(RIM, RIM)],
            dst_ref=target.at[pl.ds(to_next, RIM)],
            send_sem=sems.at[2],
            recv_sem=sems.at[3],
            device_id=((grp + 1) % regions, me),
            device_id_type=MESH,
        )
        return prev, next_

    def start_rims(copies):
        pl.when(grp > 0)(copies[0].start)
        pl.when(grp < regions - 1)(copies[1].start)

    def take_rims(copies):
        pl.when(grp < regions - 1)(copies[0].wait_recv)
        pl.when(grp > 0)(copies[1].wait_recv)

    def end_rims(copies):
        pl.when(grp > 0)(copies[0].wait_send)
        pl.when(grp < regions - 1)(copies[1].wait_send)

    terms[TAPS:] = jnp.zeros((regions * share - TAPS, 1, D), F32)
    lent[...] = dot(rows_of(halo_ref[...], ROWS), features_ref[...]).astype(BF16)
    padded[:ROWS, :] = features_ref[...]

    @pl.when(grp == 0)
    def _():
        padded[ROWS : ROWS + RIM, :] = jnp.zeros((RIM, D), BF16)
        echoed[:RIM, :] = jnp.zeros((RIM, D), BF16)

    @pl.when(grp == regions - 1)
    def _():
        padded[ROWS + RIM :, :] = jnp.zeros((RIM, D), BF16)
        echoed[RIM:, :] = jnp.zeros((RIM, D), BF16)

    def weighted(step, half, one_hot, table, first):
        span = pl.ds(pl.multiple_of(half * HALF, HALF), HALF)
        added = jnp.zeros((ROWS, HALF), F32)
        for k in range(CENTRE):
            k = step * (CENTRE + 1) + k
            picked = dot(one_hot(taps_ref[pl.ds(k, 1), :]), table[:, span])
            added = added + picked * weight_ref[pl.ds(k, 1), span]
            for part_of in range(2):
                found = picked[:, part_of * LANES : (part_of + 1) * LANES].astype(BF16)
                at = half * 2 + part_of
                picks[at, k] = found if first else picks[at, k] + found
        return added

    def from_own(half):
        span = pl.ds(pl.multiple_of(half * HALF, HALF), HALF)
        own = padded[:ROWS, span].astype(F32)
        acc[half] = own + own * weight_ref[CENTRE : CENTRE + 1, span]

        def taps(step):
            acc[half] += weighted(step, half, lambda row: rows_of(row, ROWS), padded.at[pl.ds(0, ROWS)], True)

        each(0, 2, taps)

    from_own(0)
    pl.semaphore_wait(barrier, peers - 1 + regions - 1)
    halo = rim_copies(lent, padded, halo_sems, ROWS + RIM, ROWS)
    start_rims(halo)
    send_rows[...] = rows_of(send_row, ROWS)
    send_columns[...] = columns_of(send_row, ROWS)
    curve_rows[...] = rows_of(curve_ref[...], flat)
    curve_columns[...] = columns_of(curve_ref[...], flat)
    from_own(1)
    take_rims(halo)

    def send_block(source, target, send_sem, recv_sem, lanes):
        def one(step):
            peer = (me + step) % peers
            pltpu.make_async_remote_copy(
                src_ref=source.at[peer, :, lanes],
                dst_ref=target.at[me, :, lanes],
                send_sem=send_sem,
                recv_sem=recv_sem,
                device_id=(grp, peer),
                device_id_type=MESH,
            ).start()

        each(1, peers, one)
        target[me, :, lanes] = source[me, :, lanes]

    def wait_blocks(buffer, sem, lanes):
        view = buffer.at[pl.ds(0, peers - 1), :, lanes]
        pltpu.make_async_copy(view, view, sem).wait()

    def forward(half):
        def taps(step):
            acc[half] += weighted(
                step, half, lambda row: rows_of(row - ROWS, 2 * RIM), padded.at[pl.ds(ROWS, 2 * RIM)], False
            )

        each(0, 2, taps)
        hidden = acc[half].astype(BF16)
        outgoing[half] = dot(send_rows[...], hidden).astype(BF16).reshape(peers, slots, HALF)

        def group(part_of):
            lanes = pl.ds(pl.multiple_of(part_of * LANES, LANES), LANES)
            index = half * 2 + part_of
            send_block(outgoing.at[half], incoming.at[half], out_sems.at[index], in_sems.at[index], lanes)

        each(0, 2, group)

    each(0, 2, forward)

    def attend(index):
        half = index // 2
        lanes = pl.ds(pl.multiple_of(index % 2 * LANES, LANES), LANES)
        span = pl.ds(pl.multiple_of(index * LANES, LANES), LANES)
        wait_blocks(incoming.at[half], in_sems.at[index], lanes)
        rows = incoming[half, :, :, lanes].reshape(flat, LANES)
        curve[...] = dot(curve_rows[...], rows).astype(BF16)
        grads[...] = head_grads(curve[...], cotangent_ref[:, span])
        placed = dot(curve_columns[...], grads[...]).astype(BF16)
        filled[half, :, :, lanes] = placed.reshape(peers, slots, LANES)
        send_block(filled.at[half], returned.at[half], filled_sems.at[index], returned_sems.at[index], lanes)

    each(0, 4, attend)

    def over_regions(source, target, sems):
        def one(step):
            other = (grp + step) % regions
            pltpu.make_async_remote_copy(
                src_ref=source(other),
                dst_ref=target.at[grp],
                send_sem=sems.at[0],
                recv_sem=sems.at[1],
                device_id=(other, me),
                device_id_type=MESH,
            ).start()

        each(1, regions, one)

    def wait_rows(buffer, sem, count):
        view = buffer.at[pl.ds(0, count)]
        pltpu.make_async_copy(view, view, sem).wait()

    def scatter_terms():
        over_regions(lambda other: terms.at[pl.ds(other * share, share)], parts, part_sems)

    def exchange_parts():
        parts[grp] = terms[pl.ds(grp * share, share)]
        wait_rows(parts, part_sems.at[1], regions - 1)
        mine = jnp.sum(parts[...], axis=0)
        part[...] = mine
        sums[me] = mine

        def to_peer(step):
            peer = (me + step) % peers
            pltpu.make_async_remote_copy(
                src_ref=part,
                dst_ref=sums.at[me],
                send_sem=sum_sems.at[0],
                recv_sem=sum_sems.at[1],
                device_id=(grp, peer),
                device_id_type=MESH,
            ).start()

        each(1, peers, to_peer)

    def finish_sums():
        wait_rows(sums, sum_sems.at[1], peers - 1)
        whole[grp] = jnp.sum(sums[...], axis=0)
        over_regions(lambda other: whole.at[grp], whole, whole_sems)

    def collect(index):
        half = index // 2
        lanes = pl.ds(pl.multiple_of(index % 2 * LANES, LANES), LANES)
        span = pl.ds(pl.multiple_of(index * LANES, LANES), LANES)
        wait_blocks(returned.at[half], returned_sems.at[index], lanes)
        rows = returned[half, :, :, lanes].reshape(flat, LANES)
        grad_hidden[:, span] = dot(send_columns[...], rows).astype(BF16)
        partial[...] = jnp.zeros((TAPS, 8, LANES), F32)

        def sum_terms(block):
            rows = pl.ds(pl.multiple_of(block * RIM, RIM), RIM)
            grad = grad_hidden[rows, span].astype(F32)
            for k in range(TAPS):
                found = padded[rows, span] if k == CENTRE else picks[index, k, rows, :]
                product = (grad * found.astype(F32)).reshape(RIM // 8, 8, LANES)
                partial[k] += jnp.sum(product, axis=0)

        each(0, ROWS // RIM, sum_terms)
        terms[:TAPS, :, span] = jnp.sum(partial[...], axis=1, keepdims=True)

    def end_terms():
        collect(3)
        scatter_terms()

    each(0, 3, collect)

    def backward(half):
        span = pl.ds(pl.multiple_of(half * HALF, HALF), HALF)
        grad = grad_hidden[:, span].astype(F32)
        spread[:ROWS, :] = grad + grad * weight_ref[CENTRE : CENTRE + 1, span]
        spread[ROWS:, :] = jnp.zeros((2 * RIM, HALF), F32)

        def taps(step):
            pl.when((half == 0) & (step == 1))(end_terms)
            pl.when((half == 1) & (step == 0))(exchange_parts)
            added = jnp.zeros((TABLE, HALF), F32)
            for k in range(CENTRE):
                k = step * (CENTRE + 1) + k
                landed = dot(columns_of(taps_ref[pl.ds(k, 1), :], TABLE), grad_hidden[:, span])
                added = added + landed * weight_ref[pl.ds(k, 1), span]
            spread[...] += added

        each(0, 2, taps)
        total[:, span] = spread[:ROWS, :]
        rims[:, span] = spread[ROWS:, :].astype(BF16)

    each(0, 2, backward)

    echo = rim_copies(rims, echoed, echo_sems, RIM, 0)
    start_rims(echo)
    finish_sums()
    take_rims(echo)
    out_ref[...] = (total[...] + dot(columns_of(halo_ref[...], ROWS), echoed[...])).astype(BF16)

    end_rims(halo)
    end_rims(echo)
    for half in range(2):
        for part_of in range(2):
            lanes = pl.ds(part_of * LANES, LANES)
            wait_blocks(outgoing.at[half], out_sems.at[half * 2 + part_of], lanes)
            wait_blocks(filled.at[half], filled_sems.at[half * 2 + part_of], lanes)
    wait_rows(parts, part_sems.at[0], regions - 1)
    wait_rows(sums, sum_sems.at[0], peers - 1)
    wait_rows(whole, whole_sems.at[0], regions - 1)
    wait_rows(whole, whole_sems.at[1], regions - 1)
    for k in range(TAPS):
        conv_ref[k : k + 1, :] = whole[k // share, k % share]


def hand_over(grad_ref, conv_ref, grad_out_ref, conv_out_ref):
    grad_out_ref[...] = grad_ref[...]
    conv_out_ref[...] = conv_ref[...]


def on_device(features, cotangent, conv_weight, neighbours, halo_index, send_index, curve_slot):
    peers, slots = send_index.shape[1:]
    regions = lax.axis_size("grp")
    flat = peers * slots
    share = -(-TAPS // regions)
    args = (
        neighbours.T,
        conv_weight,
        send_index.reshape(peers, slots),
        curve_slot.reshape(1, ROWS),
        halo_index,
        features,
        cotangent,
    )
    blocks = pltpu.VMEM((2, peers, slots, HALF), BF16)
    dma = pltpu.SemaphoreType.DMA
    results = pl.pallas_call(
        functools.partial(kernel, regions, peers, slots),
        out_shape=(
            jax.ShapeDtypeStruct((ROWS, D), BF16),
            jax.ShapeDtypeStruct((TAPS, D), F32),
        ),
        in_specs=[VMEM] * len(args),
        out_specs=(VMEM, VMEM),
        scratch_shapes=[
            pltpu.VMEM((TABLE, D), BF16),
            pltpu.VMEM((2 * RIM, D), BF16),
            pltpu.VMEM((flat, ROWS), BF16),
            pltpu.VMEM((ROWS, flat), BF16),
            pltpu.VMEM((ROWS, flat), BF16),
            pltpu.VMEM((flat, ROWS), BF16),
            pltpu.VMEM((2, ROWS, HALF), F32),
            pltpu.VMEM((4, TAPS, ROWS, LANES), BF16),
            blocks,
            blocks,
            pltpu.VMEM((ROWS, LANES), BF16),
            pltpu.VMEM((ROWS, LANES), BF16),
            blocks,
            blocks,
            pltpu.VMEM((ROWS, D), BF16),
            pltpu.VMEM((TABLE, HALF), F32),
            pltpu.VMEM((ROWS, D), F32),
            pltpu.VMEM((2 * RIM, D), BF16),
            pltpu.VMEM((2 * RIM, D), BF16),
            pltpu.VMEM((TAPS, 8, LANES), F32),
            pltpu.VMEM((regions * share, 1, D), F32),
            pltpu.VMEM((regions, share, 1, D), F32),
            pltpu.VMEM((share, 1, D), F32),
            pltpu.VMEM((peers, share, 1, D), F32),
            pltpu.VMEM((regions, share, 1, D), F32),
            dma((4,)),
            dma((4,)),
            dma((4,)),
            dma((4,)),
            dma((4,)),
            dma((4,)),
            dma((2,)),
            dma((2,)),
            dma((2,)),
        ],
        compiler_params=pltpu.CompilerParams(
            vmem_limit_bytes=60 * 2**20, collective_id=0, has_side_effects=True
        ),
    )(*args)
    return pl.pallas_call(
        hand_over,
        out_shape=tuple(jax.ShapeDtypeStruct(a.shape, a.dtype) for a in results),
        grid=(4,),
        in_specs=[
            pl.BlockSpec((ROWS // 4, D), lambda i: (i, 0)),
            pl.BlockSpec((TAPS, D), lambda i: (0, 0)),
        ],
        out_specs=(
            pl.BlockSpec((ROWS // 4, D), lambda i: (i, 0)),
            pl.BlockSpec((TAPS, D), lambda i: (0, 0)),
        ),
    )(*results)


def solution(mesh):
    in_specs = (
        P(("grp", "pt"), None),
        P(("grp", "pt"), None),
        P(),
        P(("grp", "pt"), None),
        P(("grp", "pt"), None),
        P(("grp", "pt"), None, None),
        P(("grp", "pt")),
    )
    out_specs = (P(("grp", "pt"), None), P())
    return jax.shard_map(
        on_device, mesh=mesh, in_specs=in_specs, out_specs=out_specs, check_vma=False
    )
```
